128 devices in a mesh: section: 2 (over core), row: 16 (over z, y), col: 4 (over x).
Axes of the slice: x: 4, y: 4, z: 4, core: 2. Of those that a mesh axis runs over, the one named last changes fastest.
Arguments:
- ends: bfloat16 [2, 2, 3152, 768], P('section', None, 'row', 'col'), may hold values from -6 to 6
- gain_attn: float32 [2, 768], P('section'), may hold values from 0.5 to 1.5
- w_qkv: bfloat16 [2, 768, 2304], P('section', 'row', 'col'), may hold values from -0.21875 to 0.21875
- w_out: bfloat16 [2, 768, 768], P('section', 'col', 'row'), may hold values from -1.75 to 1.75
- gain_ffn: float32 [2, 768], P('section'), may hold values from 0.5 to 1.5
- w_fc1: bfloat16 [768, 3072], P('row', ('section', 'col')), may hold values from -0.21875 to 0.21875
- w_fc2: bfloat16 [3072, 768], P(('section', 'col'), 'row'), may hold values from -0.15625 to 0.15625
- router: bfloat16 [768, 16], P('section'), may hold values from -0.15625 to 0.15625
- w_up: bfloat16 [16, 768, 3072], P('row', 'section', 'col'), may hold values from -0.21875 to 0.21875
- w_down: bfloat16 [16, 3072, 768], P('row', 'col', 'section'), may hold values from -1.75 to 1.75
- routes: int32 [2, 3152, 2], P(None, 'row'), may hold values from 0 to 15, all different within a row; in each aligned block of 197 rows (0 to 196, 197 to 393, ..., all dimensions but the last counted through in order) at most 40 rows name the same one
Outputs:
- ends_out: bfloat16 [2, 2, 3152, 768], P('section', None, 'row', 'col')
- grad_gain_attn: float32 [2, 768], P('section')
- grad_w_qkv: float32 [2, 768, 2304], P('section', 'row', 'col')
- grad_w_out: float32 [2, 768, 768], P('section', 'col', 'row')
- grad_gain_ffn: float32 [2, 768], P('section')
- grad_w_fc1: float32 [768, 3072], P('row', ('section', 'col'))
- grad_w_fc2: float32 [3072, 768], P(('section', 'col'), 'row')
- grad_router: float32 [768, 16], P('section')
- grad_w_up: float32 [16, 768, 3072], P('row', 'section', 'col')
- grad_w_down: float32 [16, 3072, 768], P('row', 'col', 'section')
The draws below stay inside these ranges and needn't reach their ends.
Inputs may be any that keep to these rules, and one draw needn't show every extreme that they name: `routes`: each token names 2 different experts. Among the 197 tokens of one index of row in one micro-batch (aligned blocks of 197 tokens), no expert is named more than 40 times, a bound that some block reaches in every draw.
All inputs are finite; a program needn't handle non-finite values.
Results may differ from the reference program's by a relative error of at most 0.035.
Values may be sent and summed in bfloat16 or wider, within the bound.
No kernel may reach another device: no remote copies, remote signals or barrier semaphores. Data moves between devices by JAX's collectives and lax.ppermute only.
A program may use at most 192 MiB of HBM per device.

```python
import math
import jax
import jax.numpy as jnp
import numpy as np
from jax import lax

D = 768
H = 12
HD = 64
FF = 3072
TOPK = 2
SEQ = 197
BATCHES = 2
TOK = 197
TOKENS = 3152
EXPERTS = 16
CAP = 40


def block_scale(stream_key, shape, split, least, largest):
    level, own = 1.0, jax.random.fold_in(stream_key, 6)
    for axis_at, parts in split:
        draws = jnp.exp(jax.random.uniform(jax.random.fold_in(own, axis_at), (parts,), jnp.float32, least / len(split), largest / len(split)))
        level = level * jnp.repeat(draws, shape[axis_at] // parts).reshape([-1 if axis == axis_at else 1 for axis in range(len(shape))])
    return level


def routed_block(stream_key, own, number, rows, number_of, top, limit, skew):
    sequence = jax.random.permutation(stream_key, number_of)
    crowded, usual = portions_of(number_of, rows * top, limit, skew, True), portions_of(number_of, rows * top, limit, skew, False)
    places = jnp.arange(number_of)

    def named(tallies, turn):
        used = int((tallies > 0).sum())
        fixed = max(1, used // 4)
        moved = fixed + (places - fixed + turn * (used - fixed)) % max(1, number_of - fixed)
        return jnp.zeros((number_of,), jnp.int32).at[sequence[jnp.where(places < fixed, places, moved)]].set(jnp.asarray(tallies, jnp.int32))

    tallies = jnp.where(number % 4 == 0, named(crowded, number // 4), named(usual, number - number // 4 - 1))
    mixed = jax.random.permutation(jax.random.fold_in(own, 3), number_of)
    source_of, receiver = mixed[0:number_of // 2 * 2:2], mixed[1:number_of // 2 * 2:2]
    margin = jnp.minimum(tallies[source_of] - 1, limit - tallies[receiver]) // 2
    margin = jnp.where((source_of == sequence[0]) | (receiver == sequence[0]) | (tallies[receiver] == 0), 0, jnp.maximum(margin, 0))
    moved = jax.random.randint(jax.random.fold_in(own, 4), (number_of // 2,), 0, 1 << 20) % (margin + 1)
    tallies = tallies.at[source_of].add(-moved).at[receiver].add(moved)
    labels = jnp.searchsorted(jnp.cumsum(tallies), jnp.arange(rows * top), side="right").astype(jnp.int32)
    listing = labels.reshape(top, rows).T
    listing = listing[jax.random.permutation(jax.random.fold_in(own, 1), rows)]
    turn = jax.random.randint(jax.random.fold_in(own, 2), (rows, 1), 0, top)
    return jnp.take_along_axis(listing, (jnp.arange(top)[None, :] + turn) % top, axis=1)


def portions_of(number_of, total, reach, slope, full):
    loads = [(1 << 20) // math.isqrt(standing ** slope) + 1 for standing in range(1, number_of + 1)]
    largest = reach if full else min(reach, max(-(-total // number_of), total * loads[0] // sum(loads)))
    least = 1 if total - largest >= number_of - 1 else 0
    counts, surplus = [largest] + [least] * (number_of - 1), total - largest - least * (number_of - 1)
    while surplus > 0:
        candidates = [i for i in range(1, number_of) if counts[i] < largest] or [i for i in range(1, number_of) if counts[i] < reach]
        mass, remaining = sum([loads[i] for i in candidates]), surplus
        for i in candidates:
            extra = min(reach - counts[i], max(1, remaining * loads[i] // mass), surplus)
            counts[i] = counts[i] + extra
            surplus = surplus - extra
    return np.array(counts)


def gaussian(key, extent, deviation, bound, cuts=(), held_as=jnp.bfloat16):
    level = block_scale(key, extent, cuts, -0.22, 0.18) if cuts else 1.0
    drawn = jax.random.normal(key, extent, jnp.float32) * deviation * level
    return jnp.minimum(jnp.maximum(drawn, -bound), bound).astype(held_as)


def setup_inputs(seed: int = 0) -> dict:
    key_of = jax.random.split(jax.random.key(seed), 12)
    ends = gaussian(key_of[0], (2, BATCHES, TOKENS, D), 1.0, 6.0, ((0, 2), (2, 16), (3, 4)))
    gain_attn = jnp.clip(1.0 + 0.1 * jax.random.normal(key_of[1], (2, D), jnp.float32), 0.5, 1.5)
    w_qkv = gaussian(key_of[2], (2, D, 3 * D), D ** -0.5, 0.21875, ((0, 2), (1, 16), (2, 4)))
    w_out = gaussian(key_of[3], (2, D, D), (max(D // 64, 1)) ** -0.5, 1.75, ((0, 2), (1, 4), (2, 16)))
    gain_ffn = jnp.clip(1.0 + 0.1 * jax.random.normal(key_of[4], (2, D), jnp.float32), 0.5, 1.5)
    w_fc1 = gaussian(key_of[5], (D, FF), D ** -0.5, 0.21875, ((0, 16), (1, 8)))
    w_fc2 = gaussian(key_of[6], (FF, D), (FF // 2) ** -0.5, 0.15625, ((0, 8), (1, 16)))
    router = gaussian(key_of[7], (D, EXPERTS), (2 * D) ** -0.5, 0.15625, ((0, 2),))
    w_up = gaussian(key_of[8], (EXPERTS, D, FF), D ** -0.5, 0.21875, ((0, 16), (1, 2), (2, 4)))
    w_down = gaussian(key_of[9], (EXPERTS, FF, D), (max(FF // (EXPERTS * EXPERTS), 1)) ** -0.5, 1.75, ((0, 16), (1, 4), (2, 2)))
    routes_keys = jax.random.split(jax.random.fold_in(key_of[10], 1), BATCHES * TOKENS // TOK)
    routes_turns = jax.random.permutation(jax.random.fold_in(key_of[10], 3), BATCHES * TOKENS // TOK)
    routes = jax.vmap(lambda own, number: routed_block(jax.random.fold_in(key_of[10], 2), own, number, TOK, EXPERTS, TOPK, CAP, 1))(routes_keys, routes_turns).reshape((BATCHES, TOKENS, TOPK))
    return {"ends": ends, "gain_attn": gain_attn, "w_qkv": w_qkv, "w_out": w_out, "gain_ffn": gain_ffn, "w_fc1": w_fc1, "w_fc2": w_fc2, "router": router, "w_up": w_up, "w_down": w_down, "routes": routes}


@jax.custom_vjp
def low(v):
    return lax.optimization_barrier(v.astype(jnp.bfloat16)).astype(jnp.float32)

@jax.custom_vjp
def low_back(v):
    return v

def low_keep(v):
    return (low(v), None)

def low_pass(kept, grad):
    return (grad,)

def back_keep(v):
    return (v, None)

def back_low(kept, grad):
    return (low(grad),)
low.defvjp(low_keep, low_pass)
low_back.defvjp(back_keep, back_low)
exact_mode = lax.Precision.HIGHEST

def norm_rows(values, gain):
    centre = values - lax.optimization_barrier(jnp.mean(values, axis=-1, keepdims=True))
    spread = lax.optimization_barrier(jnp.mean(centre * centre, axis=-1, keepdims=True))
    return centre * lax.rsqrt(spread + 1e-06) * gain

def product(left, right):
    return jnp.dot(left, right, precision=exact_mode)

def attention(normed, w_qkv):
    images = TOKENS // SEQ
    project = low(low_back(product(normed, w_qkv))).reshape(images, SEQ, H, 3, HD)
    queries = project[:, :, :, 0]
    keys = project[:, :, :, 1]
    values = project[:, :, :, 2]
    scores = low_back(jnp.einsum('bqhd,bkhd->bhqk', queries, keys, precision=exact_mode) * HD ** (-0.5))
    weights = low(jax.nn.softmax(scores, axis=-1))
    mixed = jnp.einsum('bhqk,bkhd->bqhd', weights, values, precision=exact_mode)
    return low(low_back(mixed)).reshape(TOKENS, D)

def attend(inputs, gain_attn, w_qkv, w_out):
    normed = low(norm_rows(inputs, gain_attn))
    branch = low_back(product(attention(normed, w_qkv), w_out))
    return inputs + branch

def dense_part(second, fc_in, fc_out):
    hidden = low_back(product(second, fc_in))
    active = low(jax.nn.gelu(hidden, approximate=False))
    return low_back(product(active, fc_out))

def expert_block(rows, up_block, down_block):
    hidden = low_back(product(rows, up_block))
    active = low(jax.nn.gelu(hidden, approximate=False))
    return low(low_back(product(active, down_block)))
expert_saved = jax.checkpoint(expert_block)

def run_expert(pieces):
    return expert_saved(pieces[0], pieces[1], pieces[2])

def expert_part(second, router, w_up, w_down, choices):
    shares = jax.nn.softmax(product(second, router), axis=-1)
    gates = jnp.take_along_axis(shares, choices, axis=1)
    blocks = TOKENS // TOK
    grouped = choices.reshape(blocks, TOK * TOPK).astype(jnp.int32)
    onehot = (grouped[:, :, None] == jnp.arange(EXPERTS, dtype=jnp.int32)[None, None, :]).astype(jnp.int32)
    placed = lax.optimization_barrier(jnp.sum((jnp.cumsum(onehot, axis=1).astype(jnp.int32) - 1) * onehot, axis=2)).astype(jnp.int32)
    rows_at = (jnp.arange(blocks, dtype=jnp.int32)[:, None] * CAP + placed).reshape(-1).astype(jnp.int32)
    experts_at = grouped.reshape(-1)
    owners = jnp.repeat(jnp.arange(TOKENS, dtype=jnp.int32), TOPK)
    buffer = jnp.zeros((EXPERTS, blocks * CAP, D), jnp.float32).at[experts_at, rows_at].set(second[owners])
    returned = lax.map(run_expert, (low_back(buffer), w_up, w_down))
    picked = returned[experts_at, rows_at].reshape(TOKENS, TOPK, D)
    return lax.optimization_barrier(jnp.sum(gates[:, :, None] * picked, axis=1))

def reference(ends, gain_attn, w_qkv, w_out, gain_ffn, w_fc1, w_fc2, router, w_up, w_down, routes):
    starts = ends[0].astype(jnp.float32)

    def relay(starts, gain_one, attn_cols, out_rows, gain_two, fc_in, fc_out, gate_table, up_blocks, down_blocks):
        outputs = []
        for batch in range(BATCHES):
            middle = attend(starts[batch], gain_one[0], attn_cols[0], out_rows[0])
            second = low(norm_rows(low(middle), gain_two[0]))
            handed = low(low_back(middle + dense_part(second, fc_in, fc_out)))
            middle = attend(handed, gain_one[1], attn_cols[1], out_rows[1])
            second = low(norm_rows(low(middle), gain_two[1]))
            outputs.append(low(middle + expert_part(second, gate_table, up_blocks, down_blocks, routes[batch])))
        return jnp.stack(outputs)
    primal, pullback = jax.vjp(relay, starts, gain_attn.astype(jnp.float32), w_qkv.astype(jnp.float32), w_out.astype(jnp.float32), gain_ffn.astype(jnp.float32), w_fc1.astype(jnp.float32), w_fc2.astype(jnp.float32), router.astype(jnp.float32), w_up.astype(jnp.float32), w_down.astype(jnp.float32))
    grads = pullback(ends[1].astype(jnp.float32))
    ends_out = jnp.stack([grads[0], primal]).astype(jnp.bfloat16)
    return (ends_out, grads[1], grads[2], grads[3], grads[4], grads[5], grads[6], grads[7], grads[8], grads[9])
```

```python
import jax
import jax.numpy as jnp
from jax import lax
from jax.sharding import PartitionSpec as P

HD = 64
SEQ = 197
CAP = 40

exact_mode = lax.Precision.HIGHEST
BF = jnp.bfloat16
F32 = jnp.float32


def swap(block):
    return lax.ppermute(block, "section", [(0, 1), (1, 0)])


def from_col(block, distance):
    return lax.ppermute(block, "col", [(i, (i + distance) % 4) for i in range(4)])


def matmul(left, right):
    return jnp.dot(left, right, preferred_element_type=F32)


def matmul_left_t(left, right):
    return lax.dot_general(left, right, (((0,), (0,)), ((), ())), preferred_element_type=F32)


def matmul_right_t(left, right):
    return lax.dot_general(left, right, (((1,), (1,)), ((), ())), preferred_element_type=F32)


def norm_parts(values):
    centre = values - jnp.mean(values, axis=-1, keepdims=True)
    spread = jnp.mean(centre * centre, axis=-1, keepdims=True)
    inverse = lax.rsqrt(spread + 1e-06)
    return centre * inverse, inverse


def norm_back(grad, gain, normed, inverse):
    scaled = grad * gain
    return inverse * (
        scaled
        - jnp.mean(scaled, axis=-1, keepdims=True)
        - normed * jnp.mean(scaled * normed, axis=-1, keepdims=True)
    )


def cdf_of(values):
    return 0.5 * (1.0 + lax.erf(values * 0.7071067811865476))


def gelu(values):
    return (values * cdf_of(values)).astype(BF)


def gelu_slope(values):
    return cdf_of(values) + values * jnp.exp(-0.5 * values * values) * 0.3989422804014327


def two_terms(values):
    upper = lax.optimization_barrier(values.astype(BF))
    lower = (values - upper.astype(F32)).astype(BF)
    return upper, lower


def col_sum(part):
    own = lax.optimization_barrier(part.astype(BF))
    parts = [own] + [from_col(own, distance) for distance in (1, 2, 3)]
    parts = [piece.astype(F32) for piece in parts]
    return (parts[0] + parts[2]) + (parts[1] + parts[3])


def row_exchange(values):
    return lax.all_to_all(values, "row", split_axis=0, concat_axis=0, tiled=True)


def heads_of(project, kind):
    tokens, width = project.shape
    return project.reshape(tokens, width // (3 * HD), 3, HD)[:, :, kind]


def shares_of(project):
    scores = jnp.einsum(
        "qhd,khd->hqk", heads_of(project, 0), heads_of(project, 1), preferred_element_type=F32
    ) * (HD ** (-0.5))
    return jax.nn.softmax(scores, axis=-1)


def body(ends, gain_attn, w_qkv, w_out, gain_ffn, w_fc1, w_fc2, router, w_up, w_down, routes):
    tokens = ends.shape[2]
    quarter = ends.shape[3]
    width = 4 * quarter
    experts = 16
    slots = experts * CAP
    first = lax.axis_index("section") == 0
    column = lax.axis_index("col")
    expert = lax.axis_index("row")

    packed = jnp.concatenate(
        [w_fc1, w_fc2.T, w_out[0].T, jnp.zeros((48, 64), BF), w_qkv[0]], axis=1
    )
    gathered = lax.all_gather(packed, ("section", "col", "row"), axis=0, tiled=True)
    gathered = gathered.reshape(2, 4, width, packed.shape[1])
    fc_in = gathered[:, :, :, :384].reshape(8, width, 384)
    fc_out_t = gathered[:, :, :, 384:768].reshape(8, width, 384)
    out_t = gathered[:, :, :, 768 : 768 + quarter]
    qkv = gathered[:, :, :, 1024:]

    kept = jnp.where(first, ends[0, 0], ends[0, 1])
    other = swap(jnp.where(first, ends[0, 1], ends[0, 0]))
    start = lax.all_gather(jnp.where(first, kept, other), "col", axis=1, tiled=True)
    cotangent = lax.all_gather(jnp.where(first, other, kept), "col", axis=1, tiled=True)
    choices = jnp.where(first, routes[0], routes[1])
    gains = [swap(gain_attn), swap(gain_ffn)]
    gain_one = [
        jnp.where(first, gain_attn[0], gains[0][0]),
        jnp.where(first, gains[0][0], gain_attn[0]),
    ]
    gain_two = [
        jnp.where(first, gain_ffn[0], gains[1][0]),
        jnp.where(first, gains[1][0], gain_ffn[0]),
    ]
    router_other = swap(router)
    gate_table = jnp.concatenate(
        [jnp.where(first, router, router_other), jnp.where(first, router_other, router)], axis=0
    )
    up_other = swap(w_up[0])
    down_other = swap(w_down[0])
    up_block = jnp.concatenate(
        [jnp.where(first, w_up[0], up_other), jnp.where(first, up_other, w_up[0])], axis=0
    )
    down_block = jnp.concatenate(
        [jnp.where(first, w_down[0], down_other), jnp.where(first, down_other, w_down[0])], axis=1
    )

    kinds = jnp.arange(experts, dtype=jnp.int32)
    hot = [(choices[:, i : i + 1] == kinds[None, :]).astype(F32) for i in range(2)]
    order = jnp.arange(tokens, dtype=jnp.int32)
    before = (order[None, :] < order[:, None]).astype(BF)
    counts = matmul(before, (hot[0] + hot[1]).astype(BF))
    places = jnp.arange(slots, dtype=jnp.int32)
    taken = []
    for i in range(2):
        target = choices[:, i] * CAP + jnp.sum(counts * hot[i], axis=1).astype(jnp.int32)
        taken.append((target[:, None] == places[None, :]).astype(BF))
    both = taken[0] + taken[1]

    grad_slots = matmul_left_t(both, cotangent).astype(BF)
    grad_slots = row_exchange(grad_slots.reshape(experts, CAP, width)).reshape(slots, width)

    def attend(values, layer):
        normed, inverse = norm_parts(values)
        attn_in = (normed * gain_one[layer]).astype(BF)
        project = jnp.concatenate(
            [matmul(attn_in, qkv[layer, k]).astype(BF) for k in range(4)], axis=1
        )
        shares = shares_of(project)
        mixed = jnp.einsum(
            "hqk,khd->qhd", shares.astype(BF), heads_of(project, 2), preferred_element_type=F32
        )
        mixed = mixed.astype(BF).reshape(tokens, width)
        middle = values + sum(
            matmul_right_t(mixed[:, k * quarter : (k + 1) * quarter], out_t[layer, k])
            for k in range(4)
        )
        normed_two, inverse_two = norm_parts(middle.astype(BF).astype(F32))
        second = (normed_two * gain_two[layer]).astype(BF)
        kept = (normed, inverse, attn_in, project, shares, mixed, normed_two, inverse_two)
        return middle, second, kept

    def attend_back(kept, layer, grad_out, grad_second):
        normed, inverse, attn_in, project, shares, mixed, normed_two, inverse_two = kept
        grad_gain_two = jnp.sum(grad_second * normed_two, axis=0)
        grad_middle = grad_out + norm_back(grad_second, gain_two[layer], normed_two, inverse_two)
        branch = grad_middle.astype(BF)
        mine = lax.dynamic_slice_in_dim(mixed, column * quarter, quarter, 1)
        grad_out_t = matmul_left_t(branch, mine)
        grad_mixed = jnp.concatenate(
            [matmul(branch, out_t[layer, k]).astype(BF) for k in range(4)], axis=1
        ).reshape(tokens, -1, HD)
        grad_shares = jnp.einsum(
            "qhd,khd->hqk", grad_mixed, heads_of(project, 2), preferred_element_type=F32
        )
        grad_values = jnp.einsum(
            "hqk,qhd->khd", shares.astype(BF), grad_mixed, preferred_element_type=F32
        )
        grad_scores = shares * (
            grad_shares - jnp.sum(grad_shares * shares, axis=-1, keepdims=True)
        )
        grad_scores = grad_scores.astype(BF)
        scale = HD ** (-0.5)
        grad_queries = scale * jnp.einsum(
            "hqk,khd->qhd", grad_scores, heads_of(project, 1), preferred_element_type=F32
        )
        grad_keys = scale * jnp.einsum(
            "hqk,qhd->khd", grad_scores, heads_of(project, 0), preferred_element_type=F32
        )
        grad_project = jnp.stack([grad_queries, grad_keys, grad_values], axis=2).astype(BF)
        grad_project = grad_project.reshape(tokens, -1)
        third = 3 * quarter
        mine = lax.dynamic_slice_in_dim(grad_project, column * third, third, 1)
        grad_qkv = matmul_left_t(attn_in, mine)
        grad_in = sum(
            matmul_right_t(grad_project[:, k * third : (k + 1) * third], qkv[layer, k])
            for k in range(4)
        )
        grad_gain_one = jnp.sum(grad_in * normed, axis=0)
        grad_values_in = grad_middle + norm_back(grad_in, gain_one[layer], normed, inverse)
        return grad_values_in, grad_qkv, grad_out_t, grad_gain_one, grad_gain_two

    middle, second, kept_first = attend(start.astype(F32), 0)
    second_first = second
    hidden = jnp.einsum("td,kdh->kth", second, fc_in, preferred_element_type=F32)
    active = gelu(hidden)
    dense = jnp.einsum("kth,kdh->td", active, fc_out_t, preferred_element_type=F32)
    handed = (middle + dense).astype(BF)

    middle, second, kept_second = attend(handed.astype(F32), 1)
    sent = matmul_left_t(both, second).astype(BF)
    rows = row_exchange(sent.reshape(experts, CAP, width)).reshape(slots, width)
    shares = jax.nn.softmax(matmul(second, gate_table), axis=-1)
    gates = [jnp.sum(shares * hot[i], axis=1) for i in range(2)]

    row_shares = jax.nn.softmax(matmul(rows, gate_table), axis=-1)
    row_gate = jnp.sum(jnp.where(kinds[None, :] == expert, row_shares, 0.0), axis=1)
    expert_hidden = matmul(rows, up_block)
    expert_active = gelu(expert_hidden)
    expert_result = matmul(expert_active, down_block)
    grad_result = (grad_slots.astype(F32) * row_gate[:, None]).astype(BF)
    grad_hidden = (matmul_right_t(grad_result, down_block) * gelu_slope(expert_hidden)).astype(BF)
    grad_rows = matmul_right_t(grad_hidden, up_block).astype(BF)
    grad_gate_slots = jnp.sum(grad_slots.astype(F32) * expert_result, axis=1)
    upper, lower = two_terms(grad_gate_slots.reshape(experts, 1, CAP))
    tail = jnp.pad(jnp.concatenate([upper, lower], axis=1), ((0, 0), (0, 6), (0, width - CAP)))
    returned = row_exchange(
        jnp.concatenate([grad_rows.reshape(experts, CAP, width), tail], axis=1)
    )
    grad_down = matmul_left_t(expert_active, grad_result)
    grad_up = matmul_left_t(rows, grad_hidden)
    result_back = row_exchange(expert_result.astype(BF).reshape(experts, CAP, width))
    result_back = result_back.reshape(slots, width)

    gate_slots = returned[:, CAP, :CAP].astype(F32) + returned[:, CAP + 1, :CAP].astype(F32)
    gate_slots = gate_slots.reshape(1, slots)
    gate_parts = jnp.stack(
        [jnp.sum(taken[i].astype(F32) * gate_slots, axis=1) for i in range(2)], axis=0
    )
    upper, lower = two_terms(gate_parts)
    tail = jnp.pad(jnp.concatenate([upper, lower], axis=0), ((0, 7), (0, width - tokens)))
    part = matmul(both, returned[:, :CAP].reshape(slots, width)).astype(BF)
    summed = col_sum(jnp.concatenate([part, tail], axis=0))
    grad_gates = [summed[tokens + i, :tokens] + summed[tokens + 2 + i, :tokens] for i in range(2)]
    weighted = grad_gates[0] * gates[0] + grad_gates[1] * gates[1]
    grad_logits = shares * (
        hot[0] * grad_gates[0][:, None] + hot[1] * grad_gates[1][:, None] - weighted[:, None]
    )
    grad_router = jnp.dot(second.astype(F32).T, grad_logits, precision=exact_mode)
    grad_second = summed[:tokens] + jnp.dot(
        grad_logits, gate_table.astype(F32).T, precision=exact_mode
    )
    grad_in, grad_qkv_b, grad_out_b, grad_gain_one_b, grad_gain_two_b = attend_back(
        kept_second, 1, cotangent.astype(F32), grad_second
    )

    picked = gates[0][:, None] * matmul(taken[0], result_back) + gates[1][:, None] * matmul(
        taken[1], result_back
    )
    picked = picked.astype(BF).reshape(tokens, 4, quarter).transpose(1, 0, 2)
    picked = lax.all_to_all(picked, "col", split_axis=0, concat_axis=0, tiled=True)
    result = lax.dynamic_slice_in_dim(middle, column * quarter, quarter, 1) + jnp.sum(
        picked.astype(F32), axis=0
    )
    result = result.astype(BF)

    grad_dense = grad_in.astype(BF)
    grad_hidden = jnp.einsum("td,kdh->kth", grad_dense, fc_out_t, preferred_element_type=F32)
    grad_hidden = (grad_hidden * gelu_slope(hidden)).astype(BF)
    grad_second = jnp.einsum("kth,kdh->td", grad_hidden, fc_in, preferred_element_type=F32)

    def own_blocks(values):
        return [
            lax.dynamic_index_in_dim(values, column + 4 * k, 0, keepdims=False) for k in range(2)
        ]

    grad_fc_in = [matmul_left_t(second_first, block) for block in own_blocks(grad_hidden)]
    grad_fc_out_t = [matmul_left_t(grad_dense, block) for block in own_blocks(active)]
    grad_in, grad_qkv_a, grad_out_a, grad_gain_one_a, grad_gain_two_a = attend_back(
        kept_first, 0, grad_in, grad_second
    )
    grad_start = lax.dynamic_slice_in_dim(grad_in, column * quarter, quarter, 1).astype(BF)

    given = swap(jnp.where(first, result, grad_start))
    ends_out = jnp.stack(
        [jnp.where(first, grad_start, given), jnp.where(first, given, result)]
    )[None]

    def both_sections(for_first, for_second):
        ours = jnp.where(first, for_first, for_second)
        theirs = swap(jnp.where(first, for_second, for_first).astype(BF))
        return ours + theirs.astype(F32)

    def over_rows(total):
        pieces = row_exchange(total.astype(BF).reshape(16, 48, total.shape[1]))
        return jnp.sum(pieces.astype(F32), axis=0)

    sum_fc = both_sections(
        jnp.concatenate([grad_fc_in[0], grad_fc_out_t[0]], axis=1),
        jnp.concatenate([grad_fc_in[1], grad_fc_out_t[1]], axis=1),
    )
    shard_fc = over_rows(sum_fc)
    sum_attn = both_sections(
        jnp.concatenate([grad_out_a, grad_qkv_a], axis=1),
        jnp.concatenate([grad_out_b, grad_qkv_b], axis=1),
    )
    shard_attn = over_rows(sum_attn)
    small = both_sections(
        jnp.concatenate(
            [grad_gain_one_a, grad_gain_two_a, grad_router[: width // 2].reshape(-1)]
        ),
        jnp.concatenate(
            [grad_gain_one_b, grad_gain_two_b, grad_router[width // 2 :].reshape(-1)]
        ),
    )
    upper, lower = two_terms(small)
    small = jnp.concatenate([upper, lower]).reshape(1, -1, 128)
    small = row_exchange(jnp.broadcast_to(small, (16,) + small.shape[1:]))
    small = jnp.sum(small.astype(F32), axis=0).reshape(2, -1)
    small = small[0] + small[1]
    sum_up = both_sections(grad_up[: width // 2], grad_up[width // 2 :])
    sum_down = both_sections(grad_down[:, : width // 2], grad_down[:, width // 2 :])
    return (
        ends_out,
        small[None, :width],
        shard_attn[None, :, quarter:],
        shard_attn[:, :quarter].T[None],
        small[None, width : 2 * width],
        shard_fc[:, :384],
        shard_fc[:, 384:].T,
        small[2 * width :].reshape(width // 2, experts),
        sum_up[None],
        sum_down[None],
    )


def solution(mesh):
    placed = (
        P("section", None, "row", "col"),
        P("section", None),
        P("section", "row", "col"),
        P("section", "col", "row"),
        P("section", None),
        P("row", ("section", "col")),
        P(("section", "col"), "row"),
        P("section", None),
        P("row", "section", "col"),
        P("row", "col", "section"),
        P(None, "row", None),
    )
    return jax.shard_map(
        body,
        mesh=mesh,
        in_specs=placed,
        out_specs=(
            P("section", None, "row", "col"),
            P("section", None),
            P("section", "row", "col"),
            P("section", "col", "row"),
            P("section", None),
            P("row", ("section", "col")),
            P(("section", "col"), "row"),
            P("section", None),
            P("row", "section", "col"),
            P("row", "col", "section"),
        ),
        check_vma=False,
    )
```

```python
import functools

import jax
import jax.numpy as jnp
from jax import lax
from jax.experimental import pallas as pl
from jax.experimental.pallas import tpu as pltpu
from jax.sharding import PartitionSpec as P

HD = 64
SEQ = 197
CAP = 40

exact_mode = lax.Precision.HIGHEST
BF = jnp.bfloat16
F32 = jnp.float32


def swap(block):
    return lax.ppermute(block, "section", [(0, 1), (1, 0)])


def from_col(block, distance):
    return lax.ppermute(block, "col", [(i, (i + distance) % 4) for i in range(4)])


def matmul(left, right):
    return jnp.dot(left, right, preferred_element_type=F32)


def matmul_left_t(left, right):
    return lax.dot_general(left, right, (((0,), (0,)), ((), ())), preferred_element_type=F32)


def matmul_right_t(left, right):
    return lax.dot_general(left, right, (((1,), (1,)), ((), ())), preferred_element_type=F32)


def norm_parts(values):
    centre = values - jnp.mean(values, axis=-1, keepdims=True)
    spread = jnp.mean(centre * centre, axis=-1, keepdims=True)
    inverse = lax.rsqrt(spread + 1e-06)
    return centre * inverse, inverse


def norm_back(grad, gain, normed, inverse):
    scaled = grad * gain
    return inverse * (
        scaled
        - jnp.mean(scaled, axis=-1, keepdims=True)
        - normed * jnp.mean(scaled * normed, axis=-1, keepdims=True)
    )


def cdf_of(values):
    return 0.5 * (1.0 + lax.erf(values * 0.7071067811865476))


def gelu(values):
    return (values * cdf_of(values)).astype(BF)


def gelu_slope(values):
    return cdf_of(values) + values * jnp.exp(-0.5 * values * values) * 0.3989422804014327


def two_terms(values):
    upper = lax.optimization_barrier(values.astype(BF))
    lower = (values - upper.astype(F32)).astype(BF)
    return upper, lower


def col_sum(part):
    own = lax.optimization_barrier(part.astype(BF))
    parts = [own] + [from_col(own, distance) for distance in (1, 2, 3)]
    parts = [piece.astype(F32) for piece in parts]
    return (parts[0] + parts[2]) + (parts[1] + parts[3])


def row_exchange(values):
    return lax.all_to_all(values, "row", split_axis=0, concat_axis=0, tiled=True)


ROWS = 256
GROUP = 192
SIDE = 768
PARAMS = pltpu.CompilerParams(vmem_limit_bytes=47 * 1024 * 1024)
SMALL = pltpu.CompilerParams(vmem_limit_bytes=24 * 1024 * 1024)


def cost(flops, size):
    return pl.CostEstimate(flops=int(flops), bytes_accessed=int(size), transcendentals=0)


def head(block, h, kind):
    at = h * GROUP + kind * HD
    return block[:, at : at + HD]


def head_shares(query, key):
    scores = matmul_right_t(query, key) * (HD ** (-0.5))
    keys = lax.broadcasted_iota(jnp.int32, scores.shape, 1)
    scores = jnp.where(keys < SEQ, scores, -1e30)
    shares = jnp.exp(scores - jnp.max(scores, axis=-1, keepdims=True))
    return shares * (1.0 / jnp.sum(shares, axis=-1, keepdims=True))


def attend_kernel(x_ref, one_ref, two_ref, w_ref, p_ref, o_ref, m_ref, mb_ref, c_ref, a_ref):
    step = pl.program_id(0)

    @pl.when(step == 0)
    def _():
        values = x_ref[...].astype(F32)
        normed, _ = norm_parts(values)
        a_ref[...] = (normed * one_ref[...]).astype(BF)
        m_ref[...] = values

    branch = 0.0
    for j in range(2):
        project = matmul(a_ref[...], w_ref[0, j]).astype(BF)
        p_ref[j] = project
        outs = [jnp.zeros((ROWS, HD), BF)]
        for h in range(3):
            shares = head_shares(head(project, h, 0), head(project, h, 1)).astype(BF)
            outs.append(matmul(shares, head(project, h, 2)).astype(BF))
        mixed = jnp.concatenate(outs, axis=1)
        o_ref[j] = mixed
        branch += matmul_right_t(mixed, w_ref[0, j, :, 512:])
    m_ref[...] += branch

    @pl.when(step == 1)
    def _():
        mb_ref[...] = m_ref[...].astype(BF)
        normed, _ = norm_parts(mb_ref[...].astype(F32))
        c_ref[...] = (normed * two_ref[...]).astype(BF)


def attend_back_kernel(
    col_ref, g_ref, d_ref, m_ref, x_ref, one_ref, two_ref, p_ref, o_ref, w_ref,
    v_ref, gw_ref, g1_ref, g2_ref, dm_ref, db_ref, acc_ref, dp_ref, a_ref,
):
    step = pl.program_id(0)

    @pl.when(step == 0)
    def _():
        normed, _ = norm_parts(x_ref[...].astype(F32))
        a_ref[...] = (normed * one_ref[...]).astype(BF)
        normed, inverse = norm_parts(m_ref[...].astype(F32))
        grad = d_ref[...]
        g2_ref[...] = jnp.sum(grad * normed, axis=0, keepdims=True)
        middle = g_ref[...].astype(F32) + norm_back(grad, two_ref[...], normed, inverse)
        dm_ref[...] = middle
        db_ref[...] = middle.astype(BF)
        acc_ref[...] = jnp.zeros_like(acc_ref)

    branch = db_ref[...]
    scale = HD ** (-0.5)
    total = 0.0
    for j in range(2):
        project = p_ref[j]
        grad_mixed = matmul(branch, w_ref[0, j, :, 512:]).astype(BF)
        grads = []
        for h in range(3):
            query, key, value = [head(project, h, kind) for kind in range(3)]
            grad_head = grad_mixed[:, (h + 1) * HD : (h + 2) * HD]
            shares = head_shares(query, key)
            grad_shares = matmul_right_t(grad_head, value)
            grad_value = matmul_left_t(shares.astype(BF), grad_head)
            grad_scores = shares * (
                grad_shares - jnp.sum(grad_shares * shares, axis=-1, keepdims=True)
            )
            grad_scores = grad_scores.astype(BF)
            grads.append((scale * matmul(grad_scores, key)).astype(BF))
            grads.append((scale * matmul_left_t(grad_scores, query)).astype(BF))
            grads.append(grad_value.astype(BF))
        grads.append(jnp.zeros((ROWS, GROUP), BF))
        grad_project = jnp.concatenate(grads, axis=1)
        dp_ref[j] = grad_project
        total += matmul_right_t(grad_project, w_ref[0, j])
    acc_ref[...] += total

    @pl.when(step == col_ref[0] // 2)
    def _():
        place = col_ref[0] % 2
        grad_project = dp_ref[place]
        gw_ref[:, :512] = matmul_left_t(a_ref[...], grad_project[:, :512]).astype(BF)
        gw_ref[:, 512:] = (
            matmul_left_t(a_ref[...], grad_project[:, 512:]) + matmul_left_t(branch, o_ref[place])
        ).astype(BF)

    @pl.when(step == 1)
    def _():
        normed, inverse = norm_parts(x_ref[...].astype(F32))
        grad = acc_ref[...]
        g1_ref[...] = jnp.sum(grad * normed, axis=0, keepdims=True)
        v_ref[...] = dm_ref[...] + norm_back(grad, one_ref[...], normed, inverse)


def dense_kernel(c_ref, m_ref, w_ref, u_ref, acc_ref):
    step = pl.program_id(0)

    @pl.when(step == 0)
    def _():
        acc_ref[...] = m_ref[...]

    total = 0.0
    for j in range(2):
        active = gelu(matmul(c_ref[...], w_ref[0, j, :, :384]))
        total += matmul_right_t(active, w_ref[0, j, :, 384:])
    acc_ref[...] += total

    @pl.when(step == 3)
    def _():
        u_ref[...] = acc_ref[...].astype(BF)


def dense_back_kernel(own_ref, g_ref, c_ref, w_ref, d_ref, gw_ref, pair_ref):
    step = pl.program_id(0)

    @pl.when(step == 0)
    def _():
        d_ref[...] = jnp.zeros_like(d_ref)

    grad = g_ref[...].astype(BF)
    total = 0.0
    for j in range(2):
        hidden = matmul(c_ref[...], w_ref[0, j, :, :384])
        active = gelu(hidden)
        grad_hidden = (matmul(grad, w_ref[0, j, :, 384:]) * gelu_slope(hidden)).astype(BF)
        total += matmul_right_t(grad_hidden, w_ref[0, j, :, :384])
        pair_ref[j, 0] = grad_hidden
        pair_ref[j, 1] = active
    d_ref[...] += total

    for place in range(2):

        @pl.when(step == own_ref[place] // 2)
        def _():
            at = own_ref[place] % 2
            gw_ref[place, :, :384] = matmul_left_t(c_ref[...], pair_ref[at, 0]).astype(BF)
            gw_ref[place, :, 384:] = matmul_left_t(grad, pair_ref[at, 1]).astype(BF)


def expert_kernel(
    me_ref, x_ref, d_ref, table_ref, up_ref, down_ref, r_ref, back_ref, a_ref, dr_ref, dz_ref
):
    rows = x_ref[...]
    wide = d_ref[...].astype(F32)
    logits = matmul(rows, table_ref[...])
    shares = jnp.exp(logits - jnp.max(logits, axis=-1, keepdims=True))
    kinds = lax.broadcasted_iota(jnp.int32, shares.shape, 1)
    chosen = jnp.sum(jnp.where(kinds == me_ref[0], shares, 0.0), axis=-1, keepdims=True)
    gate = chosen / jnp.sum(shares, axis=-1, keepdims=True)
    hidden = matmul(rows, up_ref[...])
    active = gelu(hidden)
    result = matmul(active, down_ref[...])
    grad_result = (wide * gate).astype(BF)
    grad_active = matmul_right_t(grad_result, down_ref[...])
    grad_hidden = (grad_active * gelu_slope(hidden)).astype(BF)
    grad_rows = matmul_right_t(grad_hidden, up_ref[...])
    r_ref[...] = result.astype(BF)
    a_ref[...] = active
    dr_ref[...] = grad_result
    dz_ref[...] = grad_hidden
    products = jnp.concatenate([wide * result, jnp.zeros((96, SIDE), F32)], axis=0)
    sums = lax.dot_general(
        jnp.ones((8, SIDE), F32),
        products,
        (((1,), (1,)), ((), ())),
        preferred_element_type=F32,
        precision=exact_mode,
    )
    upper = sums.astype(BF).astype(F32)
    line = lax.broadcasted_iota(jnp.int32, sums.shape, 0)
    tail = jnp.where(line == 0, upper, jnp.where(line == 1, sums - upper, 0.0))
    tail = jnp.concatenate([tail, jnp.zeros((8, SIDE - 256), F32)], axis=1)
    for j in range(4):
        piece = jnp.concatenate([grad_rows[j * CAP : (j + 1) * CAP], tail], axis=0)
        back_ref[j] = piece.astype(BF)


def run_expert(expert, rows, grad_slots, table, up_block, down_block):
    slots = rows.shape[0]
    part = slots // 4
    moving = pl.BlockSpec((part, SIDE), lambda k, *_: (k, 0))
    spec = pltpu.PrefetchScalarGridSpec(
        num_scalar_prefetch=1,
        grid=(4,),
        in_specs=[moving, moving, fixed(SIDE, 16), fixed(SIDE, SIDE), fixed(SIDE, SIDE)],
        out_specs=[
            moving,
            pl.BlockSpec((4, 48, SIDE), lambda k, *_: (k, 0, 0)),
            moving,
            moving,
            moving,
        ],
    )
    whole = jax.ShapeDtypeStruct((slots, SIDE), BF)
    return pl.pallas_call(
        expert_kernel,
        grid_spec=spec,
        out_shape=[whole, jax.ShapeDtypeStruct((16, 48, SIDE), BF), whole, whole, whole],
        compiler_params=SMALL,
        cost_estimate=cost(4e9, 1e7),
        name="expert",
    )(expert, rows, grad_slots, table, up_block, down_block)


def fixed(*shape):
    return pl.BlockSpec(shape, lambda k, *_: (0,) * len(shape))


def of_step(*shape):
    return pl.BlockSpec((2,) + shape, lambda k, *_: (k,) + (0,) * len(shape))


def run_attend(values, one, two, weights, layer):
    return pl.pallas_call(
        attend_kernel,
        grid=(2,),
        in_specs=[
            fixed(ROWS, SIDE),
            fixed(1, SIDE),
            fixed(1, SIDE),
            pl.BlockSpec((1, 2, SIDE, SIDE), lambda k: (layer, k, 0, 1)),
        ],
        out_specs=[
            of_step(ROWS, SIDE),
            of_step(ROWS, 256),
            fixed(ROWS, SIDE),
            fixed(ROWS, SIDE),
            fixed(ROWS, SIDE),
        ],
        out_shape=[
            jax.ShapeDtypeStruct((4, ROWS, SIDE), BF),
            jax.ShapeDtypeStruct((4, ROWS, 256), BF),
            jax.ShapeDtypeStruct((ROWS, SIDE), F32),
            jax.ShapeDtypeStruct((ROWS, SIDE), BF),
            jax.ShapeDtypeStruct((ROWS, SIDE), BF),
        ],
        scratch_shapes=[pltpu.VMEM((ROWS, SIDE), BF)],
        compiler_params=PARAMS,
        cost_estimate=cost(4e9, 8e6),
        name=f"attend_{layer}",
    )(values, one, two, weights)


def run_attend_back(column, grad_out, grad_second, kept, one, two, weights, layer):
    values, project, mixed, middle = kept
    spec = pltpu.PrefetchScalarGridSpec(
        num_scalar_prefetch=1,
        grid=(2,),
        in_specs=[
            fixed(ROWS, SIDE),
            fixed(ROWS, SIDE),
            fixed(ROWS, SIDE),
            fixed(ROWS, SIDE),
            fixed(1, SIDE),
            fixed(1, SIDE),
            of_step(ROWS, SIDE),
            of_step(ROWS, 256),
            pl.BlockSpec((1, 2, SIDE, SIDE), lambda k, *_: (layer, k, 0, 1)),
        ],
        out_specs=[
            fixed(ROWS, SIDE),
            fixed(SIDE, SIDE),
            fixed(1, SIDE),
            fixed(1, SIDE),
        ],
        scratch_shapes=[
            pltpu.VMEM((ROWS, SIDE), F32),
            pltpu.VMEM((ROWS, SIDE), BF),
            pltpu.VMEM((ROWS, SIDE), F32),
            pltpu.VMEM((2, ROWS, SIDE), BF),
            pltpu.VMEM((ROWS, SIDE), BF),
        ],
    )
    return pl.pallas_call(
        attend_back_kernel,
        grid_spec=spec,
        out_shape=[
            jax.ShapeDtypeStruct((ROWS, SIDE), F32),
            jax.ShapeDtypeStruct((SIDE, SIDE), BF),
            jax.ShapeDtypeStruct((1, SIDE), F32),
            jax.ShapeDtypeStruct((1, SIDE), F32),
        ],
        compiler_params=PARAMS,
        cost_estimate=cost(8e9, 1e7),
        name=f"attend_back_{layer}",
    )(column, grad_out, grad_second, middle, values, one, two, project, mixed, weights)


def dense_block():
    return pl.BlockSpec((1, 2, SIDE, SIDE), lambda k, *_: (k // 2, k % 2, 0, 0))


def run_dense(second, middle, weights):
    return pl.pallas_call(
        dense_kernel,
        grid=(4,),
        in_specs=[fixed(ROWS, SIDE), fixed(ROWS, SIDE), dense_block()],
        out_specs=fixed(ROWS, SIDE),
        out_shape=jax.ShapeDtypeStruct((ROWS, SIDE), BF),
        scratch_shapes=[pltpu.VMEM((ROWS, SIDE), F32)],
        compiler_params=PARAMS,
        cost_estimate=cost(4e9, 1.2e7),
        name="dense",
    )(second, middle, weights)


def run_dense_back(own, grad, second, weights):
    spec = pltpu.PrefetchScalarGridSpec(
        num_scalar_prefetch=1,
        grid=(4,),
        in_specs=[fixed(ROWS, SIDE), fixed(ROWS, SIDE), dense_block()],
        out_specs=[fixed(ROWS, SIDE), fixed(2, SIDE, SIDE)],
        scratch_shapes=[pltpu.VMEM((2, 2, ROWS, 384), BF)],
    )
    return pl.pallas_call(
        dense_back_kernel,
        grid_spec=spec,
        out_shape=[
            jax.ShapeDtypeStruct((ROWS, SIDE), F32),
            jax.ShapeDtypeStruct((2, SIDE, SIDE), BF),
        ],
        compiler_params=PARAMS,
        cost_estimate=cost(8e9, 1.4e7),
        name="dense_back",
    )(own, grad, second, weights)


def body(ends, gain_attn, w_qkv, w_out, gain_ffn, w_fc1, w_fc2, router, w_up, w_down, routes):
    tokens = ends.shape[2]
    quarter = ends.shape[3]
    width = 4 * quarter
    half = width // 2
    experts = 16
    slots = experts * CAP
    extra = ROWS - tokens
    tie = lax.optimization_barrier
    section = lax.axis_index("section").astype(jnp.int32)
    first = section == 0
    column = lax.axis_index("col").astype(jnp.int32)
    expert = lax.axis_index("row").astype(jnp.int32)

    def by_section(mine, theirs):
        return jnp.where(first, mine, theirs), jnp.where(first, theirs, mine)

    packed = jnp.concatenate([w_fc1, w_fc2.T, w_qkv[0], w_out[0].T], axis=1)
    gathered = lax.all_gather(packed, ("section", "col", "row"), axis=0, tiled=True)
    gathered = gathered.reshape(2, 4, width, 2 * width)

    kept = jnp.where(first, ends[0, 0], ends[0, 1])
    other = swap(jnp.where(first, ends[0, 1], ends[0, 0]))
    start, cotangent = by_section(kept, other)
    start = lax.all_gather(start, "col", axis=1, tiled=True)
    start, cotangent = tie((start, cotangent))
    cotangent = lax.all_gather(cotangent, "col", axis=1, tiled=True)
    start = jnp.pad(start, ((0, extra), (0, 0)))
    cotangent = jnp.pad(cotangent, ((0, extra), (0, 0)))
    choices = jnp.where(first, routes[0], routes[1])
    choices = jnp.pad(choices, ((0, extra), (0, 0)), constant_values=-1)
    gain_one = by_section(gain_attn, swap(gain_attn))
    gain_two = by_section(gain_ffn, swap(gain_ffn))
    gate_table = jnp.concatenate(by_section(router, swap(router)), axis=0)
    up_block = jnp.concatenate(by_section(w_up[0], swap(w_up[0])), axis=0)
    down_block = jnp.concatenate(by_section(w_down[0], swap(w_down[0])), axis=1)

    kinds = jnp.arange(experts, dtype=jnp.int32)
    hot = [(choices[:, i : i + 1] == kinds[None, :]).astype(F32) for i in range(2)]
    order = jnp.arange(ROWS, dtype=jnp.int32)
    before = (order[None, :] < order[:, None]).astype(BF)
    counts = matmul(before, (hot[0] + hot[1]).astype(BF))
    places = jnp.arange(slots, dtype=jnp.int32)
    taken = []
    targets_back = []
    for i in range(2):
        slot = jnp.sum(counts * hot[i], axis=1).astype(jnp.int32)
        target = choices[:, i] * CAP + slot
        targets_back.append(choices[:, i] * 48 + slot)
        taken.append((target[:, None] == places[None, :]).astype(BF))
    both = taken[0] + taken[1]
    places = jnp.arange(experts * 48, dtype=jnp.int32)
    both_back = sum((at[:, None] == places[None, :]).astype(BF) for at in targets_back)

    grad_slots = matmul_left_t(both, cotangent).astype(BF)
    grad_slots = row_exchange(grad_slots.reshape(experts, CAP, width)).reshape(slots, width)
    gathered, grad_slots, up_block, down_block = tie((gathered, grad_slots, up_block, down_block))

    project, mixed, middle, middle_low, second = run_attend(
        start, gain_one[0], gain_two[0], gathered, 0
    )
    kept_first = (start, project, mixed, middle_low)
    second_first = second
    handed = run_dense(second, middle, gathered)
    project, mixed, middle, middle_low, second = run_attend(
        handed, gain_one[1], gain_two[1], gathered, 1
    )
    kept_second = (handed, project, mixed, middle_low)
    sent = matmul_left_t(both, second).astype(BF)
    rows = row_exchange(sent.reshape(experts, CAP, width)).reshape(slots, width)
    shares = jax.nn.softmax(matmul(second, gate_table), axis=-1)
    gates = [jnp.sum(shares * hot[i], axis=1) for i in range(2)]

    expert_result, grad_rows, expert_active, grad_result, grad_hidden = run_expert(
        expert[None], rows, grad_slots, gate_table, up_block, down_block
    )
    returned = row_exchange(grad_rows)
    grad_down = matmul_left_t(expert_active, grad_result).astype(BF)
    grad_up = matmul_left_t(rows, grad_hidden).astype(BF)

    def pair_sum(mine, theirs):
        return mine.astype(F32) + swap(theirs).astype(F32)

    sum_up = pair_sum(*by_section(grad_up[:half], grad_up[half:]))
    sum_down = pair_sum(*by_section(grad_down[:, :half], grad_down[:, half:]))
    returned, expert_result, sum_up, sum_down = tie((returned, expert_result, sum_up, sum_down))

    gate_slots = lax.dynamic_slice(
        returned, (0, CAP, (expert % 4) * CAP), (experts, 2, CAP)
    ).astype(F32)
    gate_slots = (gate_slots[:, 0] + gate_slots[:, 1]).reshape(1, slots)
    gate_parts = jnp.stack(
        [jnp.sum(taken[i].astype(F32) * gate_slots, axis=1)[:tokens] for i in range(2)], axis=0
    )
    upper, lower = two_terms(gate_parts)
    tail = jnp.pad(jnp.concatenate([upper, lower], axis=0), ((0, 7), (0, width - tokens)))
    part = matmul(both_back, returned.reshape(experts * 48, width)).astype(BF)[:tokens]
    summed = col_sum(jnp.concatenate([part, tail], axis=0))
    summed, expert_result = tie((summed, expert_result))
    result_back = row_exchange(expert_result.reshape(experts, CAP, width))
    result_back = result_back.reshape(slots, width)
    grad_gates = [
        jnp.pad(summed[tokens + i, :tokens] + summed[tokens + 2 + i, :tokens], (0, extra))
        for i in range(2)
    ]
    weighted = grad_gates[0] * gates[0] + grad_gates[1] * gates[1]
    grad_logits = shares * (
        hot[0] * grad_gates[0][:, None] + hot[1] * grad_gates[1][:, None] - weighted[:, None]
    )
    grad_router = lax.dot_general(
        grad_logits, second.astype(F32), (((0,), (0,)), ((), ())), precision=exact_mode
    )
    grad_second = jnp.pad(summed[:tokens], ((0, extra), (0, 0))) + lax.dot_general(
        grad_logits, gate_table.astype(F32), (((1,), (1,)), ((), ())), precision=exact_mode
    )
    grad_in, grad_attn_b, grad_one_b, grad_two_b = run_attend_back(
        column[None], cotangent, grad_second, kept_second, gain_one[1], gain_two[1], gathered, 1
    )

    def paired(values):
        ours, theirs = by_section(values[:, :half], values[:, half:])
        return (ours.astype(F32) + swap(theirs).astype(F32)).astype(BF).reshape(16, 48, half)

    def spread(gain):
        upper, lower = two_terms(gain.reshape(2, half))
        return jnp.concatenate([upper, lower], axis=0)

    def to_rows(pieces, small):
        small = jnp.broadcast_to(small[None], (16,) + small.shape)
        return jnp.concatenate([pieces, small], axis=1)

    def total(values):
        return jnp.sum(values.astype(F32), axis=0)

    def gain_total(values):
        values = total(values)
        return values[:2] + values[2:]

    ours, theirs = by_section(grad_router[:, :half], grad_router[:, half:])
    router_half = (ours + swap(theirs)).astype(BF)
    small = jnp.concatenate([spread(grad_one_b), spread(grad_two_b), router_half], axis=0)
    load = to_rows(paired(grad_attn_b), small)
    load, grad_in, result_back = tie((load, grad_in, result_back))
    sums_b = row_exchange(load)

    def columns_of(values, at):
        return lax.dynamic_slice_in_dim(values, at * quarter, quarter, 1)[:tokens]

    def own_columns(values):
        return columns_of(values, column)

    own = jnp.stack([section * 4 + column, (1 - section) * 4 + column])
    grad_second, grad_fc = run_dense_back(own, grad_in, second_first, gathered)
    grad_fc, sums_b = tie((grad_fc, sums_b))
    fc = (grad_fc[0].astype(F32) + swap(grad_fc[1]).astype(F32)).astype(BF)
    fc = jnp.concatenate(
        [fc[:, :half].reshape(16, 48, half), fc[:, half:].reshape(16, 48, half)], axis=1
    )
    grad_second, fc = tie((grad_second, fc))
    sums_c = row_exchange(fc)
    grad_in, grad_attn_a, grad_one_a, grad_two_a = run_attend_back(
        column[None], grad_in, grad_second, kept_first, gain_one[0], gain_two[0], gathered, 0
    )
    grad_attn_a, sums_c = tie((grad_attn_a, sums_c))
    grad_start = own_columns(grad_in).astype(BF)
    small = jnp.concatenate([spread(grad_one_a), spread(grad_two_a)], axis=0)
    load = to_rows(paired(grad_attn_a), small)
    load, sums_c, result_back = tie((load, sums_c, result_back))
    sums_a = row_exchange(load)

    picked = gates[0][:, None] * matmul(taken[0], result_back) + gates[1][:, None] * matmul(
        taken[1], result_back
    )
    result = own_columns(middle) + own_columns(picked)
    for distance in (1, 2, 3):
        sent = columns_of(picked, (column + distance) % 4).astype(BF)
        result += from_col(sent, distance).astype(F32)
    result = result.astype(BF)


    shard_b, shard_a = total(sums_b[:, :48]), total(sums_a[:, :48])
    gains_b = jnp.concatenate([gain_total(sums_b[:, 48:52]), gain_total(sums_b[:, 52:56])], axis=0)
    gains_a = jnp.concatenate(
        [gain_total(sums_a[:, 48:52]), gain_total(sums_a[:, 52:56])], axis=0
    )
    mine, theirs = by_section(
        jnp.concatenate([shard_a, gains_a], axis=0), jnp.concatenate([shard_b, gains_b], axis=0)
    )
    theirs = swap(theirs)
    left, right = by_section(mine[:48], theirs[:48])
    gains = mine[48:] + theirs[48:]
    given = swap(jnp.where(first, result, grad_start))
    ends_out = jnp.stack(
        [jnp.where(first, grad_start, given), jnp.where(first, given, result)]
    )[None]
    return (
        ends_out,
        gains[:2].reshape(1, width),
        jnp.concatenate([left, right[:, : half - quarter]], axis=1)[None],
        right[:, half - quarter :].T[None],
        gains[2:].reshape(1, width),
        total(sums_c[:, :48]),
        total(sums_c[:, 48:]).T,
        total(sums_b[:, 56:]).T,
        sum_up[None],
        sum_down[None],
    )


def solution(mesh):
    placed = (
        P("section", None, "row", "col"),
        P("section", None),
        P("section", "row", "col"),
        P("section", "col", "row"),
        P("section", None),
        P("row", ("section", "col")),
        P(("section", "col"), "row"),
        P("section", None),
        P("row", "section", "col"),
        P("row", "col", "section"),
        P(None, "row", None),
    )
    return jax.shard_map(
        body,
        mesh=mesh,
        in_specs=placed,
        out_specs=(
            P("section", None, "row", "col"),
            P("section", None),
            P("section", "row", "col"),
            P("section", "col", "row"),
            P("section", None),
            P("row", ("section", "col")),
            P(("section", "col"), "row"),
            P("section", None),
            P("row", "section", "col"),
            P("row", "col", "section"),
        ),
        check_vma=False,
    )
```

```python
import jax
import jax.numpy as jnp
from jax import lax
from jax.experimental import pallas as pl
from jax.experimental.pallas import tpu as pltpu
from jax.sharding import PartitionSpec as P

HD = 64
SEQ = 197
CAP = 40

exact_mode = lax.Precision.HIGHEST
BF = jnp.bfloat16
F32 = jnp.float32


def swap(block):
    return lax.ppermute(block, "section", [(0, 1), (1, 0)])


def from_col(block, distance):
    return lax.ppermute(block, "col", [(i, (i + distance) % 4) for i in range(4)])


def matmul(left, right):
    return jnp.dot(left, right, preferred_element_type=F32)


def matmul_left_t(left, right):
    return lax.dot_general(left, right, (((0,), (0,)), ((), ())), preferred_element_type=F32)


def matmul_right_t(left, right):
    return lax.dot_general(left, right, (((1,), (1,)), ((), ())), preferred_element_type=F32)


def norm_parts(values):
    centre = values - jnp.mean(values, axis=-1, keepdims=True)
    spread = jnp.mean(centre * centre, axis=-1, keepdims=True)
    inverse = lax.rsqrt(spread + 1e-06)
    return centre * inverse, inverse


def norm_back(grad, gain, normed, inverse):
    scaled = grad * gain
    return inverse * (
        scaled
        - jnp.mean(scaled, axis=-1, keepdims=True)
        - normed * jnp.mean(scaled * normed, axis=-1, keepdims=True)
    )


def cdf_of(values):
    return 0.5 * (1.0 + lax.erf(values * 0.7071067811865476))


def gelu(values):
    return (values * cdf_of(values)).astype(BF)


def gelu_slope(values):
    return cdf_of(values) + values * jnp.exp(-0.5 * values * values) * 0.3989422804014327


def two_terms(values):
    upper = lax.optimization_barrier(values.astype(BF))
    lower = (values - upper.astype(F32)).astype(BF)
    return upper, lower


def col_sum(part):
    own = lax.optimization_barrier(part.astype(BF))
    parts = [own] + [from_col(own, distance) for distance in (1, 2, 3)]
    parts = [piece.astype(F32) for piece in parts]
    return (parts[0] + parts[2]) + (parts[1] + parts[3])


def row_exchange(values):
    return lax.all_to_all(values, "row", split_axis=0, concat_axis=0, tiled=True)


ROWS = 256
GROUP = 192
SIDE = 768
PARAMS = pltpu.CompilerParams(vmem_limit_bytes=47 * 1024 * 1024)
SMALL = pltpu.CompilerParams(vmem_limit_bytes=24 * 1024 * 1024)


def cost(flops, size):
    return pl.CostEstimate(flops=int(flops), bytes_accessed=int(size), transcendentals=0)


def head(block, h, kind):
    at = h * GROUP + kind * HD
    return block[:, at : at + HD]


def key_shares(query, key):
    scores = matmul_right_t(key, query) * (HD ** (-0.5))
    keys = lax.broadcasted_iota(jnp.int32, scores.shape, 0)
    scores = jnp.where(keys < SEQ, scores, -1e30)
    shares = jnp.exp(scores - jnp.max(scores, axis=0, keepdims=True))
    return shares * (1.0 / jnp.sum(shares, axis=0, keepdims=True))


def attend_kernel(x_ref, one_ref, two_ref, w_ref, p_ref, o_ref, m_ref, mb_ref, c_ref, a_ref):
    step = pl.program_id(0)

    @pl.when(step == 0)
    def _():
        values = x_ref[...].astype(F32)
        normed, _ = norm_parts(values)
        a_ref[...] = (normed * one_ref[...]).astype(BF)
        m_ref[...] = values

    branch = 0.0
    for j in range(2):
        project = matmul(a_ref[...], w_ref[0, j]).astype(BF)
        p_ref[j] = project
        outs = [jnp.zeros((ROWS, HD), BF)]
        for h in range(3):
            shares = key_shares(head(project, h, 0), head(project, h, 1)).astype(BF)
            outs.append(matmul(head(project, h, 2).T, shares).astype(BF).T)
        mixed = jnp.concatenate(outs, axis=1)
        o_ref[j] = mixed
        branch += matmul_right_t(mixed, w_ref[0, j, :, 512:])
    m_ref[...] += branch

    @pl.when(step == 1)
    def _():
        mb_ref[...] = m_ref[...].astype(BF)
        normed, _ = norm_parts(mb_ref[...].astype(F32))
        c_ref[...] = (normed * two_ref[...]).astype(BF)


def attend_back_kernel(
    col_ref, g_ref, d_ref, m_ref, x_ref, one_ref, two_ref, p_ref, o_ref, w_ref,
    v_ref, gw_ref, g1_ref, g2_ref, dm_ref, db_ref, acc_ref, dp_ref, a_ref,
):
    step = pl.program_id(0)

    @pl.when(step == 0)
    def _():
        normed, _ = norm_parts(x_ref[...].astype(F32))
        a_ref[...] = (normed * one_ref[...]).astype(BF)
        normed, inverse = norm_parts(m_ref[...].astype(F32))
        grad = d_ref[...]
        g2_ref[...] = jnp.sum(grad * normed, axis=0, keepdims=True)
        middle = g_ref[...].astype(F32) + norm_back(grad, two_ref[...], normed, inverse)
        dm_ref[...] = middle
        db_ref[...] = middle.astype(BF)
        acc_ref[...] = jnp.zeros_like(acc_ref)

    branch = db_ref[...]
    scale = HD ** (-0.5)
    total = 0.0
    for j in range(2):
        project = p_ref[j]
        grad_mixed = matmul(branch, w_ref[0, j, :, 512:]).astype(BF)
        grads = []
        for h in range(3):
            query, key, value = [head(project, h, kind) for kind in range(3)]
            grad_head = grad_mixed[:, (h + 1) * HD : (h + 2) * HD]
            shares = key_shares(query, key)
            grad_shares = matmul_right_t(value, grad_head)
            grad_value = matmul(shares.astype(BF), grad_head)
            grad_scores = shares * (
                grad_shares - jnp.sum(grad_shares * shares, axis=0, keepdims=True)
            )
            grad_scores = grad_scores.astype(BF)
            grads.append((scale * matmul(key.T, grad_scores)).astype(BF).T)
            grads.append((scale * matmul(grad_scores, query)).astype(BF))
            grads.append(grad_value.astype(BF))
        grads.append(jnp.zeros((ROWS, GROUP), BF))
        grad_project = jnp.concatenate(grads, axis=1)
        dp_ref[j] = grad_project
        total += matmul_right_t(grad_project, w_ref[0, j])
    acc_ref[...] += total

    @pl.when(step == col_ref[0] // 2)
    def _():
        place = col_ref[0] % 2
        grad_project = dp_ref[place]
        gw_ref[:, :512] = matmul_left_t(a_ref[...], grad_project[:, :512]).astype(BF)
        gw_ref[:, 512:] = (
            matmul_left_t(a_ref[...], grad_project[:, 512:]) + matmul_left_t(branch, o_ref[place])
        ).astype(BF)

    @pl.when(step == 1)
    def _():
        normed, inverse = norm_parts(x_ref[...].astype(F32))
        grad = acc_ref[...]
        g1_ref[...] = jnp.sum(grad * normed, axis=0, keepdims=True)
        v_ref[...] = dm_ref[...] + norm_back(grad, one_ref[...], normed, inverse)


def dense_kernel(c_ref, m_ref, w_ref, u_ref, acc_ref):
    step = pl.program_id(0)

    @pl.when(step == 0)
    def _():
        acc_ref[...] = m_ref[...]

    total = 0.0
    for j in range(2):
        active = gelu(matmul(c_ref[...], w_ref[0, j, :, :384]))
        total += matmul_right_t(active, w_ref[0, j, :, 384:])
    acc_ref[...] += total

    @pl.when(step == 3)
    def _():
        u_ref[...] = acc_ref[...].astype(BF)


def dense_back_kernel(own_ref, g_ref, c_ref, w_ref, d_ref, gw_ref, pair_ref):
    step = pl.program_id(0)

    @pl.when(step == 0)
    def _():
        d_ref[...] = jnp.zeros_like(d_ref)

    grad = g_ref[...].astype(BF)
    total = 0.0
    for j in range(2):
        hidden = matmul(c_ref[...], w_ref[0, j, :, :384])
        active = gelu(hidden)
        grad_hidden = (matmul(grad, w_ref[0, j, :, 384:]) * gelu_slope(hidden)).astype(BF)
        total += matmul_right_t(grad_hidden, w_ref[0, j, :, :384])
        pair_ref[j, 0] = grad_hidden
        pair_ref[j, 1] = active
    d_ref[...] += total

    for place in range(2):

        @pl.when(step == own_ref[place] // 2)
        def _():
            at = own_ref[place] % 2
            gw_ref[place, :, :384] = matmul_left_t(c_ref[...], pair_ref[at, 0]).astype(BF)
            gw_ref[place, :, 384:] = matmul_left_t(grad, pair_ref[at, 1]).astype(BF)


def expert_kernel(
    me_ref, x_ref, d_ref, table_ref, up_ref, down_ref, r_ref, back_ref, a_ref, dr_ref, dz_ref
):
    rows = x_ref[...]
    wide = d_ref[...].astype(F32)
    logits = matmul(rows, table_ref[...])
    shares = jnp.exp(logits - jnp.max(logits, axis=-1, keepdims=True))
    kinds = lax.broadcasted_iota(jnp.int32, shares.shape, 1)
    chosen = jnp.sum(jnp.where(kinds == me_ref[0], shares, 0.0), axis=-1, keepdims=True)
    gate = chosen / jnp.sum(shares, axis=-1, keepdims=True)
    hidden = matmul(rows, up_ref[...])
    active = gelu(hidden)
    result = matmul(active, down_ref[...])
    grad_result = (wide * gate).astype(BF)
    grad_active = matmul_right_t(grad_result, down_ref[...])
    grad_hidden = (grad_active * gelu_slope(hidden)).astype(BF)
    grad_rows = matmul_right_t(grad_hidden, up_ref[...])
    r_ref[...] = result.astype(BF)
    a_ref[...] = active
    dr_ref[...] = grad_result
    dz_ref[...] = grad_hidden
    products = wide * result
    products = sum(products[:, k * 128 : (k + 1) * 128] for k in range(SIDE // 128))
    products = jnp.concatenate([products, jnp.zeros((96, 128), F32)], axis=0)
    sums = lax.dot_general(
        jnp.ones((8, 128), F32),
        products,
        (((1,), (1,)), ((), ())),
        preferred_element_type=F32,
        precision=exact_mode,
    )
    upper = sums.astype(BF).astype(F32)
    line = lax.broadcasted_iota(jnp.int32, sums.shape, 0)
    tail = jnp.where(line == 0, upper, jnp.where(line == 1, sums - upper, 0.0))
    tail = jnp.concatenate([tail, jnp.zeros((8, SIDE - 256), F32)], axis=1)
    for j in range(4):
        piece = jnp.concatenate([grad_rows[j * CAP : (j + 1) * CAP], tail], axis=0)
        back_ref[j] = piece.astype(BF)


def run_expert(expert, rows, grad_slots, table, up_block, down_block):
    slots = rows.shape[0]
    part = slots // 4
    moving = pl.BlockSpec((part, SIDE), lambda k, *_: (k, 0))
    spec = pltpu.PrefetchScalarGridSpec(
        num_scalar_prefetch=1,
        grid=(4,),
        in_specs=[moving, moving, fixed(SIDE, 16), fixed(SIDE, SIDE), fixed(SIDE, SIDE)],
        out_specs=[
            moving,
            pl.BlockSpec((4, 48, SIDE), lambda k, *_: (k, 0, 0)),
            moving,
            moving,
            moving,
        ],
    )
    whole = pltpu.HBM((slots, SIDE), BF)
    return pl.pallas_call(
        expert_kernel,
        grid_spec=spec,
        out_shape=[whole, jax.ShapeDtypeStruct((16, 48, SIDE), BF), whole, whole, whole],
        compiler_params=SMALL,
        cost_estimate=cost(4e9, 1e7),
        name="expert",
    )(expert, rows, in_place(grad_slots), table, in_place(up_block), in_place(down_block))


def in_place(value):
    return pltpu.with_memory_space_constraint(value, pltpu.HBM)


def fixed(*shape):
    return pl.BlockSpec(shape, lambda k, *_: (0,) * len(shape))


def of_step(*shape):
    return pl.BlockSpec((2,) + shape, lambda k, *_: (k,) + (0,) * len(shape))


def run_attend(values, one, two, weights, layer):
    return pl.pallas_call(
        attend_kernel,
        grid=(2,),
        in_specs=[
            fixed(ROWS, SIDE),
            fixed(1, SIDE),
            fixed(1, SIDE),
            pl.BlockSpec((1, 2, SIDE, SIDE), lambda k: (layer, k, 0, 1)),
        ],
        out_specs=[
            of_step(ROWS, SIDE),
            of_step(ROWS, 256),
            fixed(ROWS, SIDE),
            fixed(ROWS, SIDE),
            fixed(ROWS, SIDE),
        ],
        out_shape=[
            pltpu.HBM((4, ROWS, SIDE), BF),
            pltpu.HBM((4, ROWS, 256), BF),
            jax.ShapeDtypeStruct((ROWS, SIDE), F32),
            pltpu.HBM((ROWS, SIDE), BF),
            jax.ShapeDtypeStruct((ROWS, SIDE), BF),
        ],
        scratch_shapes=[pltpu.VMEM((ROWS, SIDE), BF)],
        compiler_params=PARAMS,
        cost_estimate=cost(4e9, 8e6),
        name=f"attend_{layer}",
    )(values, one, two, weights)


def run_attend_back(column, grad_out, grad_second, kept, one, two, weights, layer):
    if layer == 0:
        kept = [in_place(value) for value in kept]
        grad_out, grad_second = in_place(grad_out), in_place(grad_second)
    values, project, mixed, middle = kept
    spec = pltpu.PrefetchScalarGridSpec(
        num_scalar_prefetch=1,
        grid=(2,),
        in_specs=[
            fixed(ROWS, SIDE),
            fixed(ROWS, SIDE),
            fixed(ROWS, SIDE),
            fixed(ROWS, SIDE),
            fixed(1, SIDE),
            fixed(1, SIDE),
            of_step(ROWS, SIDE),
            of_step(ROWS, 256),
            pl.BlockSpec((1, 2, SIDE, SIDE), lambda k, *_: (layer, k, 0, 1)),
        ],
        out_specs=[
            fixed(ROWS, SIDE),
            fixed(SIDE, SIDE),
            fixed(1, SIDE),
            fixed(1, SIDE),
        ],
        scratch_shapes=[
            pltpu.VMEM((ROWS, SIDE), F32),
            pltpu.VMEM((ROWS, SIDE), BF),
            pltpu.VMEM((ROWS, SIDE), F32),
            pltpu.VMEM((2, ROWS, SIDE), BF),
            pltpu.VMEM((ROWS, SIDE), BF),
        ],
    )
    return pl.pallas_call(
        attend_back_kernel,
        grid_spec=spec,
        out_shape=[
            pltpu.HBM((ROWS, SIDE), F32),
            jax.ShapeDtypeStruct((SIDE, SIDE), BF),
            jax.ShapeDtypeStruct((1, SIDE), F32),
            jax.ShapeDtypeStruct((1, SIDE), F32),
        ],
        compiler_params=PARAMS,
        cost_estimate=cost(8e9, 1e7),
        name=f"attend_back_{layer}",
    )(column, grad_out, grad_second, middle, values, one, two, project, mixed, weights)


def dense_block():
    return pl.BlockSpec((1, 2, SIDE, SIDE), lambda k, *_: (k // 2, k % 2, 0, 0))


def run_dense(second, middle, weights):
    return pl.pallas_call(
        dense_kernel,
        grid=(4,),
        in_specs=[fixed(ROWS, SIDE), fixed(ROWS, SIDE), dense_block()],
        out_specs=fixed(ROWS, SIDE),
        out_shape=jax.ShapeDtypeStruct((ROWS, SIDE), BF),
        scratch_shapes=[pltpu.VMEM((ROWS, SIDE), F32)],
        compiler_params=PARAMS,
        cost_estimate=cost(4e9, 1.2e7),
        name="dense",
    )(second, middle, weights)


def run_dense_back(own, grad, second, weights):
    spec = pltpu.PrefetchScalarGridSpec(
        num_scalar_prefetch=1,
        grid=(4,),
        in_specs=[fixed(ROWS, SIDE), fixed(ROWS, SIDE), dense_block()],
        out_specs=[fixed(ROWS, SIDE), fixed(2, SIDE, SIDE)],
        scratch_shapes=[pltpu.VMEM((2, 2, ROWS, 384), BF)],
    )
    return pl.pallas_call(
        dense_back_kernel,
        grid_spec=spec,
        out_shape=[
            pltpu.HBM((ROWS, SIDE), F32),
            jax.ShapeDtypeStruct((2, SIDE, SIDE), BF),
        ],
        compiler_params=PARAMS,
        cost_estimate=cost(8e9, 1.4e7),
        name="dense_back",
    )(own, in_place(grad), in_place(second), weights)


def body(ends, gain_attn, w_qkv, w_out, gain_ffn, w_fc1, w_fc2, router, w_up, w_down, routes):
    tokens = ends.shape[2]
    quarter = ends.shape[3]
    width = 4 * quarter
    half = width // 2
    experts = 16
    slots = experts * CAP
    extra = ROWS - tokens
    tie = lax.optimization_barrier
    section = lax.axis_index("section").astype(jnp.int32)
    first = section == 0
    column = lax.axis_index("col").astype(jnp.int32)
    expert = lax.axis_index("row").astype(jnp.int32)

    def by_section(mine, theirs):
        return jnp.where(first, mine, theirs), jnp.where(first, theirs, mine)

    packed = jnp.concatenate([w_fc1, w_fc2.T, w_qkv[0], w_out[0].T], axis=1)
    gathered = lax.all_gather(packed, ("section", "col", "row"), axis=0, tiled=True)
    gathered = gathered.reshape(2, 4, width, 2 * width)

    kept = jnp.where(first, ends[0, 0], ends[0, 1])
    other = swap(jnp.where(first, ends[0, 1], ends[0, 0]))
    start, cotangent = by_section(kept, other)
    start = lax.all_gather(start, "col", axis=1, tiled=True)
    start, cotangent = tie((start, cotangent))
    cotangent = lax.all_gather(cotangent, "col", axis=1, tiled=True)
    start = jnp.pad(start, ((0, extra), (0, 0)))
    cotangent = jnp.pad(cotangent, ((0, extra), (0, 0)))
    choices = jnp.where(first, routes[0], routes[1])
    choices = jnp.pad(choices, ((0, extra), (0, 0)), constant_values=-1)
    gain_one = by_section(gain_attn, swap(gain_attn))
    gain_two = by_section(gain_ffn, swap(gain_ffn))
    gate_table = jnp.concatenate(by_section(router, swap(router)), axis=0)
    up_block = jnp.concatenate(by_section(w_up[0], swap(w_up[0])), axis=0)
    down_block = jnp.concatenate(by_section(w_down[0], swap(w_down[0])), axis=1)

    kinds = jnp.arange(experts, dtype=jnp.int32)
    hot = [(choices[:, i : i + 1] == kinds[None, :]).astype(F32) for i in range(2)]
    order = jnp.arange(ROWS, dtype=jnp.int32)
    before = (order[None, :] < order[:, None]).astype(BF)
    counts = matmul(before, (hot[0] + hot[1]).astype(BF))
    places = jnp.arange(slots, dtype=jnp.int32)
    taken = []
    targets_back = []
    for i in range(2):
        slot = jnp.sum(counts * hot[i], axis=1).astype(jnp.int32)
        target = choices[:, i] * CAP + slot
        targets_back.append(choices[:, i] * 48 + slot)
        taken.append((target[:, None] == places[None, :]).astype(BF))
    both = taken[0] + taken[1]
    places = jnp.arange(experts * 48, dtype=jnp.int32)
    both_back = sum((at[:, None] == places[None, :]).astype(BF) for at in targets_back)

    grad_slots = matmul_left_t(both, cotangent).astype(BF)
    grad_slots = row_exchange(grad_slots.reshape(experts, CAP, width)).reshape(slots, width)
    gathered, grad_slots, up_block, down_block = tie((gathered, grad_slots, up_block, down_block))

    project, mixed, middle, middle_low, second = run_attend(
        start, gain_one[0], gain_two[0], gathered, 0
    )
    kept_first = (start, project, mixed, middle_low)
    second_first = second
    handed = run_dense(second, middle, gathered)
    project, mixed, middle, middle_low, second = run_attend(
        handed, gain_one[1], gain_two[1], gathered, 1
    )
    kept_second = (handed, project, mixed, middle_low)
    sent = matmul_left_t(both, second).astype(BF)
    rows = row_exchange(sent.reshape(experts, CAP, width)).reshape(slots, width)
    shares = jax.nn.softmax(matmul(second, gate_table), axis=-1)
    gates = [jnp.sum(shares * hot[i], axis=1) for i in range(2)]

    expert_result, grad_rows, expert_active, grad_result, grad_hidden = run_expert(
        expert[None], rows, grad_slots, gate_table, up_block, down_block
    )
    returned = row_exchange(grad_rows)
    grad_down = matmul_left_t(expert_active, grad_result).astype(BF)
    grad_up = matmul_left_t(rows, grad_hidden).astype(BF)

    def paired(ours, theirs):
        return ours, swap(theirs)

    returned, expert_result, grad_up, grad_down = tie(
        (returned, expert_result, grad_up, grad_down)
    )
    result_back = row_exchange(expert_result.reshape(experts, CAP, width))
    result_back = result_back.reshape(slots, width)

    gate_slots = lax.dynamic_slice(
        returned, (0, CAP, (expert % 4) * CAP), (experts, 2, CAP)
    ).astype(F32)
    gate_slots = (gate_slots[:, 0] + gate_slots[:, 1]).reshape(1, slots)
    gate_parts = jnp.stack(
        [jnp.sum(taken[i].astype(F32) * gate_slots, axis=1)[:tokens] for i in range(2)], axis=0
    )
    upper, lower = two_terms(gate_parts)
    tail = jnp.pad(jnp.concatenate([upper, lower], axis=0), ((0, 7), (0, width - tokens)))
    part = matmul(both_back, returned.reshape(experts * 48, width)).astype(BF)[:tokens]
    summed = col_sum(jnp.concatenate([part, tail], axis=0))
    up_pair = paired(*by_section(grad_up[:half], grad_up[half:]))
    down_pair = paired(*by_section(grad_down[:, :half], grad_down[:, half:]))
    summed, up_pair, down_pair = tie((summed, up_pair, down_pair))
    grad_gates = [
        jnp.pad(summed[tokens + i, :tokens] + summed[tokens + 2 + i, :tokens], (0, extra))
        for i in range(2)
    ]
    weighted = grad_gates[0] * gates[0] + grad_gates[1] * gates[1]
    grad_logits = shares * (
        hot[0] * grad_gates[0][:, None] + hot[1] * grad_gates[1][:, None] - weighted[:, None]
    )
    grad_router = lax.dot_general(
        grad_logits, second.astype(F32), (((0,), (0,)), ((), ())), precision=exact_mode
    )
    grad_second = jnp.pad(summed[:tokens], ((0, extra), (0, 0))) + lax.dot_general(
        grad_logits, gate_table.astype(F32), (((1,), (1,)), ((), ())), precision=exact_mode
    )
    grad_in, grad_attn_b, grad_one_b, grad_two_b = run_attend_back(
        column[None], cotangent, grad_second, kept_second, gain_one[1], gain_two[1], gathered, 1
    )

    def joined(ours, theirs):
        return (ours.astype(F32) + theirs.astype(F32)).astype(BF).reshape(16, 48, half)

    def spread(gain):
        upper, lower = two_terms(gain.reshape(2, half))
        return jnp.concatenate([upper, lower], axis=0)

    def to_rows(pieces, small):
        small = jnp.broadcast_to(small[None], (16,) + small.shape)
        return jnp.concatenate([pieces, small], axis=1)

    def total(values):
        return jnp.sum(values.astype(F32), axis=0)

    def gain_total(values):
        values = total(values)
        return values[:2] + values[2:]

    ours, theirs = by_section(grad_router[:, :half], grad_router[:, half:])
    router_half = (ours + swap(theirs)).astype(BF)
    small = jnp.concatenate([spread(grad_one_b), spread(grad_two_b), router_half], axis=0)
    load = to_rows(joined(*paired(*by_section(grad_attn_b[:, :half], grad_attn_b[:, half:]))), small)
    load, grad_in, result_back = tie((load, grad_in, result_back))
    sums_b = row_exchange(load)

    def columns_of(values, at):
        return lax.dynamic_slice_in_dim(values, at * quarter, quarter, 1)[:tokens]

    def own_columns(values):
        return columns_of(values, column)

    own = jnp.stack([section * 4 + column, (1 - section) * 4 + column])
    grad_second, grad_fc = run_dense_back(own, grad_in, second_first, gathered)
    grad_fc, sums_b = tie((grad_fc, sums_b))
    ours, theirs = grad_fc[0], swap(grad_fc[1])
    fc = (ours.astype(F32) + theirs.astype(F32)).astype(BF).reshape(16, 48, width)
    grad_second, fc, up_pair, down_pair = tie((grad_second, fc, up_pair, down_pair))
    sum_up = up_pair[0].astype(F32) + up_pair[1].astype(F32)
    sum_down = down_pair[0].astype(F32) + down_pair[1].astype(F32)
    sums_c = row_exchange(fc)
    grad_in, grad_attn_a, grad_one_a, grad_two_a = run_attend_back(
        column[None], grad_in, grad_second, kept_first, gain_one[0], gain_two[0], gathered, 0
    )
    grad_attn_a, sums_c, sum_up, sum_down = tie((grad_attn_a, sums_c, sum_up, sum_down))
    grad_start = own_columns(grad_in).astype(BF)
    small = jnp.concatenate([spread(grad_one_a), spread(grad_two_a)], axis=0)
    load = to_rows(joined(*paired(*by_section(grad_attn_a[:, :half], grad_attn_a[:, half:]))), small)
    load, sums_c, result_back = tie((load, sums_c, result_back))
    sums_a = row_exchange(load)

    picked = gates[0][:, None] * matmul(taken[0], result_back) + gates[1][:, None] * matmul(
        taken[1], result_back
    )
    result = own_columns(middle) + own_columns(picked)
    for distance in (1, 2, 3):
        sent = columns_of(picked, (column + distance) % 4).astype(BF)
        result += from_col(sent, distance).astype(F32)
    result = result.astype(BF)


    shard_b, shard_a = total(sums_b[:, :48]), total(sums_a[:, :48])
    gains_b = jnp.concatenate([gain_total(sums_b[:, 48:52]), gain_total(sums_b[:, 52:56])], axis=0)
    gains_a = jnp.concatenate(
        [gain_total(sums_a[:, 48:52]), gain_total(sums_a[:, 52:56])], axis=0
    )
    mine, theirs = by_section(
        jnp.concatenate([shard_a, gains_a], axis=0), jnp.concatenate([shard_b, gains_b], axis=0)
    )
    theirs = swap(theirs)
    left, right = by_section(mine[:48], theirs[:48])
    gains = mine[48:] + theirs[48:]
    given = swap(jnp.where(first, result, grad_start))
    ends_out = jnp.stack(
        [jnp.where(first, grad_start, given), jnp.where(first, given, result)]
    )[None]
    return (
        ends_out,
        gains[:2].reshape(1, width),
        jnp.concatenate([left, right[:, : half - quarter]], axis=1)[None],
        right[:, half - quarter :].T[None],
        gains[2:].reshape(1, width),
        total(sums_c[:, :, :half]),
        total(sums_c[:, :, half:]).T,
        total(sums_b[:, 56:]).T,
        sum_up[None],
        sum_down[None],
    )


def solution(mesh):
    placed = (
        P("section", None, "row", "col"),
        P("section", None),
        P("section", "row", "col"),
        P("section", "col", "row"),
        P("section", None),
        P("row", ("section", "col")),
        P(("section", "col"), "row"),
        P("section", None),
        P("row", "section", "col"),
        P("row", "col", "section"),
        P(None, "row", None),
    )
    return jax.shard_map(
        body,
        mesh=mesh,
        in_specs=placed,
        out_specs=(
            P("section", None, "row", "col"),
            P("section", None),
            P("section", "row", "col"),
            P("section", "col", "row"),
            P("section", None),
            P("row", ("section", "col")),
            P(("section", "col"), "row"),
            P("section", None),
            P("row", "section", "col"),
            P("row", "col", "section"),
        ),
        check_vma=False,
    )
```

```python
import jax
import jax.numpy as jnp
from jax import lax
from jax.experimental import pallas as pl
from jax.experimental.pallas import tpu as pltpu
from jax.sharding import PartitionSpec as P

HD = 64
SEQ = 197
CAP = 40

exact_mode = lax.Precision.HIGHEST
BF = jnp.bfloat16
F32 = jnp.float32


def swap(block):
    return lax.ppermute(block, "section", [(0, 1), (1, 0)])


def from_col(block, distance):
    return lax.ppermute(block, "col", [(i, (i + distance) % 4) for i in range(4)])


def matmul(left, right):
    return jnp.dot(left, right, preferred_element_type=F32)


def matmul_left_t(left, right):
    return lax.dot_general(left, right, (((0,), (0,)), ((), ())), preferred_element_type=F32)


def matmul_right_t(left, right):
    return lax.dot_general(left, right, (((1,), (1,)), ((), ())), preferred_element_type=F32)


def norm_parts(values):
    centre = values - jnp.mean(values, axis=-1, keepdims=True)
    spread = jnp.mean(centre * centre, axis=-1, keepdims=True)
    inverse = lax.rsqrt(spread + 1e-06)
    return centre * inverse, inverse


def norm_back(grad, gain, normed, inverse):
    scaled = grad * gain
    return inverse * (
        scaled
        - jnp.mean(scaled, axis=-1, keepdims=True)
        - normed * jnp.mean(scaled * normed, axis=-1, keepdims=True)
    )


def cdf_of(values):
    return 0.5 * (1.0 + lax.erf(values * 0.7071067811865476))


def gelu(values):
    return (values * cdf_of(values)).astype(BF)


def gelu_slope(values):
    return cdf_of(values) + values * jnp.exp(-0.5 * values * values) * 0.3989422804014327


def two_terms(values):
    upper = lax.optimization_barrier(values.astype(BF))
    lower = (values - upper.astype(F32)).astype(BF)
    return upper, lower


def col_sum(part):
    own = lax.optimization_barrier(part.astype(BF))
    parts = [own] + [from_col(own, distance) for distance in (1, 2, 3)]
    parts = [piece.astype(F32) for piece in parts]
    return (parts[0] + parts[2]) + (parts[1] + parts[3])


def row_exchange(values):
    return lax.all_to_all(values, "row", split_axis=0, concat_axis=0, tiled=True)


ROWS = 208
IMAGES = 8
GROUP = 192
SIDE = 768
PARAMS = pltpu.CompilerParams(vmem_limit_bytes=47 * 1024 * 1024)
SMALL = pltpu.CompilerParams(vmem_limit_bytes=24 * 1024 * 1024)


def cost(flops, size):
    return pl.CostEstimate(flops=int(flops), bytes_accessed=int(size), transcendentals=0)


def head(block, h, kind):
    at = h * GROUP + kind * HD
    return block[:, at : at + HD]


def key_shares(query, key):
    scores = matmul_right_t(key, query) * (HD ** (-0.5))
    keys = lax.broadcasted_iota(jnp.int32, scores.shape, 0)
    scores = jnp.where(keys < SEQ, scores, -1e30)
    shares = jnp.exp(scores - jnp.max(scores, axis=0, keepdims=True))
    return shares * (1.0 / jnp.sum(shares, axis=0, keepdims=True))


def attend_kernel(x_ref, one_ref, two_ref, w_ref, p_ref, o_ref, m_ref, mb_ref, c_ref, a_ref):
    step = pl.program_id(0)

    @pl.when(step == 0)
    def _():
        values = x_ref[...].astype(F32)
        normed, _ = norm_parts(values)
        a_ref[...] = (normed * one_ref[...]).astype(BF)
        m_ref[...] = values

    branch = 0.0
    for j in range(2):
        project = matmul(a_ref[...], w_ref[0, j]).astype(BF)
        p_ref[j] = project
        outs = [jnp.zeros((ROWS, HD), BF)]
        for h in range(3):
            shares = key_shares(head(project, h, 0), head(project, h, 1)).astype(BF)
            outs.append(matmul(head(project, h, 2).T, shares).astype(BF).T)
        mixed = jnp.concatenate(outs, axis=1)
        o_ref[j] = mixed
        branch += matmul_right_t(mixed, w_ref[0, j, :, 512:])
    m_ref[...] += branch

    @pl.when(step == 1)
    def _():
        mb_ref[...] = m_ref[...].astype(BF)
        normed, _ = norm_parts(mb_ref[...].astype(F32))
        c_ref[...] = (normed * two_ref[...]).astype(BF)


def attend_back_kernel(
    col_ref, g_ref, d_ref, m_ref, x_ref, one_ref, two_ref, p_ref, o_ref, w_ref,
    v_ref, ours_ref, theirs_ref, g1_ref, g2_ref, dm_ref, db_ref, acc_ref, dp_ref, a_ref,
):
    step = pl.program_id(0)

    @pl.when(step == 0)
    def _():
        normed, _ = norm_parts(x_ref[...].astype(F32))
        a_ref[...] = (normed * one_ref[...]).astype(BF)
        normed, inverse = norm_parts(m_ref[...].astype(F32))
        grad = d_ref[...]
        g2_ref[...] = jnp.sum(grad * normed, axis=0, keepdims=True)
        middle = g_ref[...].astype(F32) + norm_back(grad, two_ref[...], normed, inverse)
        dm_ref[...] = middle
        db_ref[...] = middle.astype(BF)
        acc_ref[...] = jnp.zeros_like(acc_ref)

    branch = db_ref[...]
    scale = HD ** (-0.5)
    total = 0.0
    for j in range(2):
        project = p_ref[j]
        grad_mixed = matmul(branch, w_ref[0, j, :, 512:]).astype(BF)
        grads = []
        for h in range(3):
            query, key, value = [head(project, h, kind) for kind in range(3)]
            grad_head = grad_mixed[:, (h + 1) * HD : (h + 2) * HD]
            shares = key_shares(query, key)
            grad_shares = matmul_right_t(value, grad_head)
            grad_value = matmul(shares.astype(BF), grad_head)
            grad_scores = shares * (
                grad_shares - jnp.sum(grad_shares * shares, axis=0, keepdims=True)
            )
            grad_scores = grad_scores.astype(BF)
            grads.append((scale * matmul(key.T, grad_scores)).astype(BF).T)
            grads.append((scale * matmul(grad_scores, query)).astype(BF))
            grads.append(grad_value.astype(BF))
        grads.append(jnp.zeros((ROWS, GROUP), BF))
        grad_project = jnp.concatenate(grads, axis=1)
        dp_ref[j] = grad_project
        total += matmul_right_t(grad_project, w_ref[0, j])
    acc_ref[...] += total

    @pl.when(step == col_ref[0] // 2)
    def _():
        place = col_ref[0] % 2
        grad_project = dp_ref[place]
        left = matmul_left_t(a_ref[...], grad_project[:, :512])
        right = matmul_left_t(a_ref[...], grad_project[:, 512:])
        right += matmul_left_t(branch, o_ref[place])
        low = left[:, :384].astype(BF)
        high = jnp.concatenate([left[:, 384:], right], axis=1).astype(BF)

        @pl.when(col_ref[1] == 0)
        def _():
            ours_ref[...] = low
            theirs_ref[...] = high

        @pl.when(col_ref[1] != 0)
        def _():
            ours_ref[...] = high
            theirs_ref[...] = low

    @pl.when(step == 1)
    def _():
        normed, inverse = norm_parts(x_ref[...].astype(F32))
        grad = acc_ref[...]
        g1_ref[...] = jnp.sum(grad * normed, axis=0, keepdims=True)
        v_ref[...] = dm_ref[...] + norm_back(grad, one_ref[...], normed, inverse)


def dense_kernel(c_ref, m_ref, w_ref, u_ref, acc_ref):
    step = pl.program_id(0)

    @pl.when(step == 0)
    def _():
        acc_ref[...] = m_ref[...]

    total = 0.0
    for j in range(2):
        active = gelu(matmul(c_ref[...], w_ref[0, j, :, :384]))
        total += matmul_right_t(active, w_ref[0, j, :, 384:])
    acc_ref[...] += total

    @pl.when(step == 3)
    def _():
        u_ref[...] = acc_ref[...].astype(BF)


def dense_back_kernel(own_ref, g_ref, c_ref, w_ref, d_ref, ours_ref, theirs_ref, pair_ref):
    step = pl.program_id(0)

    @pl.when(step == 0)
    def _():
        d_ref[...] = jnp.zeros_like(d_ref)

    grad = g_ref[...].astype(BF)
    total = 0.0
    for j in range(2):
        hidden = matmul(c_ref[...], w_ref[0, j, :, :384])
        active = gelu(hidden)
        grad_hidden = (matmul(grad, w_ref[0, j, :, 384:]) * gelu_slope(hidden)).astype(BF)
        total += matmul_right_t(grad_hidden, w_ref[0, j, :, :384])
        pair_ref[j, 0] = grad_hidden
        pair_ref[j, 1] = active
    d_ref[...] += total

    for place in range(2):

        @pl.when(step == own_ref[place] // 2)
        def _():
            at = own_ref[place] % 2
            gw_ref = (ours_ref, theirs_ref)[place]
            gw_ref[:, :384] = matmul_left_t(c_ref[...], pair_ref[at, 0]).astype(BF)
            gw_ref[:, 384:] = matmul_left_t(grad, pair_ref[at, 1]).astype(BF)


def expert_kernel(
    me_ref, x_ref, d_ref, table_ref, up_ref, down_ref, r_ref, back_ref, a_ref, dr_ref, dz_ref
):
    rows = x_ref[...]
    wide = d_ref[...].astype(F32)
    logits = matmul(rows, table_ref[...])
    shares = jnp.exp(logits - jnp.max(logits, axis=-1, keepdims=True))
    kinds = lax.broadcasted_iota(jnp.int32, shares.shape, 1)
    chosen = jnp.sum(jnp.where(kinds == me_ref[0], shares, 0.0), axis=-1, keepdims=True)
    gate = chosen / jnp.sum(shares, axis=-1, keepdims=True)
    hidden = matmul(rows, up_ref[...])
    active = gelu(hidden)
    result = matmul(active, down_ref[...])
    grad_result = (wide * gate).astype(BF)
    grad_active = matmul_right_t(grad_result, down_ref[...])
    grad_hidden = (grad_active * gelu_slope(hidden)).astype(BF)
    grad_rows = matmul_right_t(grad_hidden, up_ref[...])
    r_ref[...] = result.astype(BF)
    a_ref[...] = active
    dr_ref[...] = grad_result
    dz_ref[...] = grad_hidden
    products = wide * result
    products = sum(products[:, k * 128 : (k + 1) * 128] for k in range(SIDE // 128))
    products = jnp.concatenate([products, jnp.zeros((384 - IMAGES * CAP, 128), F32)], axis=0)
    sums = lax.dot_general(
        jnp.ones((8, 128), F32),
        products,
        (((1,), (1,)), ((), ())),
        preferred_element_type=F32,
        precision=exact_mode,
    )
    upper = sums.astype(BF).astype(F32)
    line = lax.broadcasted_iota(jnp.int32, sums.shape, 0)
    tail = jnp.where(line == 0, upper, jnp.where(line == 1, sums - upper, 0.0))
    tail = jnp.concatenate([tail, jnp.zeros((8, SIDE - 384), F32)], axis=1)
    for j in range(IMAGES):
        piece = jnp.concatenate([grad_rows[j * CAP : (j + 1) * CAP], tail], axis=0)
        back_ref[j] = piece.astype(BF)


def run_expert(expert, rows, grad_slots, table, up_block, down_block):
    slots = rows.shape[0]
    part = IMAGES * CAP
    moving = pl.BlockSpec((part, SIDE), lambda k, *_: (k, 0))
    spec = pltpu.PrefetchScalarGridSpec(
        num_scalar_prefetch=1,
        grid=(slots // part,),
        in_specs=[moving, moving, fixed(SIDE, 16), fixed(SIDE, SIDE), fixed(SIDE, SIDE)],
        out_specs=[
            moving,
            pl.BlockSpec((IMAGES, 48, SIDE), lambda k, *_: (k, 0, 0)),
            moving,
            moving,
            moving,
        ],
    )
    whole = pltpu.HBM((slots, SIDE), BF)
    return pl.pallas_call(
        expert_kernel,
        grid_spec=spec,
        out_shape=[whole, jax.ShapeDtypeStruct((16, 48, SIDE), BF), whole, whole, whole],
        compiler_params=SMALL,
        cost_estimate=cost(4e9, 1e7),
        name="expert",
    )(expert, rows, in_place(grad_slots), table, in_place(up_block), in_place(down_block))


def in_place(value):
    return pltpu.with_memory_space_constraint(value, pltpu.HBM)


def fixed(*shape):
    return pl.BlockSpec(shape, lambda k, *_: (0,) * len(shape))


def of_step(*shape):
    return pl.BlockSpec((2,) + shape, lambda k, *_: (k,) + (0,) * len(shape))


def run_attend(values, one, two, weights, layer):
    return pl.pallas_call(
        attend_kernel,
        grid=(2,),
        in_specs=[
            fixed(ROWS, SIDE),
            fixed(1, SIDE),
            fixed(1, SIDE),
            pl.BlockSpec((1, 2, SIDE, SIDE), lambda k: (layer, k, 0, 1)),
        ],
        out_specs=[
            of_step(ROWS, SIDE),
            of_step(ROWS, 256),
            fixed(ROWS, SIDE),
            fixed(ROWS, SIDE),
            fixed(ROWS, SIDE),
        ],
        out_shape=[
            pltpu.HBM((4, ROWS, SIDE), BF),
            pltpu.HBM((4, ROWS, 256), BF),
            jax.ShapeDtypeStruct((ROWS, SIDE), F32),
            pltpu.HBM((ROWS, SIDE), BF),
            jax.ShapeDtypeStruct((ROWS, SIDE), BF),
        ],
        scratch_shapes=[pltpu.VMEM((ROWS, SIDE), BF)],
        compiler_params=PARAMS,
        cost_estimate=cost(4e9, 8e6),
        name=f"attend_{layer}",
    )(values, one, two, weights)


def run_attend_back(column, grad_out, grad_second, kept, one, two, weights, layer):
    if layer == 0:
        kept = [in_place(value) for value in kept]
        grad_out, grad_second = in_place(grad_out), in_place(grad_second)
    values, project, mixed, middle = kept
    spec = pltpu.PrefetchScalarGridSpec(
        num_scalar_prefetch=1,
        grid=(2,),
        in_specs=[
            fixed(ROWS, SIDE),
            fixed(ROWS, SIDE),
            fixed(ROWS, SIDE),
            fixed(ROWS, SIDE),
            fixed(1, SIDE),
            fixed(1, SIDE),
            of_step(ROWS, SIDE),
            of_step(ROWS, 256),
            pl.BlockSpec((1, 2, SIDE, SIDE), lambda k, *_: (layer, k, 0, 1)),
        ],
        out_specs=[
            fixed(ROWS, SIDE),
            fixed(SIDE, 384),
            fixed(SIDE, 384),
            fixed(1, SIDE),
            fixed(1, SIDE),
        ],
        scratch_shapes=[
            pltpu.VMEM((ROWS, SIDE), F32),
            pltpu.VMEM((ROWS, SIDE), BF),
            pltpu.VMEM((ROWS, SIDE), F32),
            pltpu.VMEM((2, ROWS, SIDE), BF),
            pltpu.VMEM((ROWS, SIDE), BF),
        ],
    )
    return pl.pallas_call(
        attend_back_kernel,
        grid_spec=spec,
        out_shape=[
            pltpu.HBM((ROWS, SIDE), F32),
            jax.ShapeDtypeStruct((SIDE, 384), BF),
            jax.ShapeDtypeStruct((SIDE, 384), BF),
            jax.ShapeDtypeStruct((1, SIDE), F32),
            jax.ShapeDtypeStruct((1, SIDE), F32),
        ],
        compiler_params=PARAMS,
        cost_estimate=cost(8e9, 1e7),
        name=f"attend_back_{layer}",
    )(column, grad_out, grad_second, middle, values, one, two, project, mixed, weights)


def dense_block():
    return pl.BlockSpec((1, 2, SIDE, SIDE), lambda k, *_: (k // 2, k % 2, 0, 0))


def run_dense(second, middle, weights):
    return pl.pallas_call(
        dense_kernel,
        grid=(4,),
        in_specs=[fixed(ROWS, SIDE), fixed(ROWS, SIDE), dense_block()],
        out_specs=fixed(ROWS, SIDE),
        out_shape=jax.ShapeDtypeStruct((ROWS, SIDE), BF),
        scratch_shapes=[pltpu.VMEM((ROWS, SIDE), F32)],
        compiler_params=PARAMS,
        cost_estimate=cost(4e9, 1.2e7),
        name="dense",
    )(second, middle, weights)


def run_dense_back(own, grad, second, weights):
    spec = pltpu.PrefetchScalarGridSpec(
        num_scalar_prefetch=1,
        grid=(4,),
        in_specs=[fixed(ROWS, SIDE), fixed(ROWS, SIDE), dense_block()],
        out_specs=[fixed(ROWS, SIDE), fixed(SIDE, SIDE), fixed(SIDE, SIDE)],
        scratch_shapes=[pltpu.VMEM((2, 2, ROWS, 384), BF)],
    )
    return pl.pallas_call(
        dense_back_kernel,
        grid_spec=spec,
        out_shape=[
            pltpu.HBM((ROWS, SIDE), F32),
            jax.ShapeDtypeStruct((SIDE, SIDE), BF),
            jax.ShapeDtypeStruct((SIDE, SIDE), BF),
        ],
        compiler_params=PARAMS,
        cost_estimate=cost(8e9, 1.4e7),
        name="dense_back",
    )(own, in_place(grad), in_place(second), weights)


def body(ends, gain_attn, w_qkv, w_out, gain_ffn, w_fc1, w_fc2, router, w_up, w_down, routes):
    tokens = ends.shape[2]
    quarter = ends.shape[3]
    width = 4 * quarter
    half = width // 2
    experts = 16
    slots = experts * CAP
    extra = ROWS - tokens
    tie = lax.optimization_barrier
    section = lax.axis_index("section").astype(jnp.int32)
    first = section == 0
    column = lax.axis_index("col").astype(jnp.int32)
    expert = lax.axis_index("row").astype(jnp.int32)
    place = jnp.stack([column, section])

    def by_section(mine, theirs):
        return jnp.where(first, mine, theirs), jnp.where(first, theirs, mine)

    packed = jnp.concatenate([w_fc1, w_fc2.T, w_qkv[0], w_out[0].T], axis=1)
    gathered = lax.all_gather(packed, ("section", "col", "row"), axis=0, tiled=True)
    gathered = gathered.reshape(2, 4, width, 2 * width)

    kept = jnp.where(first, ends[0, 0], ends[0, 1])
    other = swap(jnp.where(first, ends[0, 1], ends[0, 0]))
    start, cotangent = by_section(kept, other)
    start = lax.all_gather(start, "col", axis=1, tiled=True)
    start, cotangent = tie((start, cotangent))
    cotangent = lax.all_gather(cotangent, "col", axis=1, tiled=True)
    start = jnp.pad(start, ((0, extra), (0, 0)))
    cotangent = jnp.pad(cotangent, ((0, extra), (0, 0)))
    choices = jnp.where(first, routes[0], routes[1])
    choices = jnp.pad(choices, ((0, extra), (0, 0)), constant_values=-1)
    gain_one = by_section(gain_attn, swap(gain_attn))
    gain_two = by_section(gain_ffn, swap(gain_ffn))
    gate_table = jnp.concatenate(by_section(router, swap(router)), axis=0)
    up_block = jnp.concatenate(by_section(w_up[0], swap(w_up[0])), axis=0)
    down_block = jnp.concatenate(by_section(w_down[0], swap(w_down[0])), axis=1)

    kinds = jnp.arange(experts, dtype=jnp.int32)
    hot = [(choices[:, i : i + 1] == kinds[None, :]).astype(F32) for i in range(2)]
    order = jnp.arange(ROWS, dtype=jnp.int32)
    before = (order[None, :] < order[:, None]).astype(BF)
    counts = matmul(before, (hot[0] + hot[1]).astype(BF))
    places = jnp.arange(slots, dtype=jnp.int32)
    taken = []
    targets_back = []
    for i in range(2):
        slot = jnp.sum(counts * hot[i], axis=1).astype(jnp.int32)
        target = choices[:, i] * CAP + slot
        targets_back.append(choices[:, i] * 48 + slot)
        taken.append((target[:, None] == places[None, :]).astype(BF))
    both = taken[0] + taken[1]
    places = jnp.arange(experts * 48, dtype=jnp.int32)
    both_back = sum((at[:, None] == places[None, :]).astype(BF) for at in targets_back)

    grad_slots = matmul_left_t(both, cotangent).astype(BF)
    grad_slots = row_exchange(grad_slots.reshape(experts, CAP, width)).reshape(slots, width)
    gathered, grad_slots, up_block, down_block = tie((gathered, grad_slots, up_block, down_block))

    project, mixed, middle, middle_low, second = run_attend(
        start, gain_one[0], gain_two[0], gathered, 0
    )
    kept_first = (start, project, mixed, middle_low)
    second_first = second
    handed = run_dense(second, middle, gathered)
    project, mixed, middle, middle_low, second = run_attend(
        handed, gain_one[1], gain_two[1], gathered, 1
    )
    kept_second = (handed, project, mixed, middle_low)
    sent = matmul_left_t(both, second).astype(BF)
    rows = row_exchange(sent.reshape(experts, CAP, width)).reshape(slots, width)
    shares = jax.nn.softmax(matmul(second, gate_table), axis=-1)
    gates = [jnp.sum(shares * hot[i], axis=1) for i in range(2)]

    expert_result, grad_rows, expert_active, grad_result, grad_hidden = run_expert(
        expert[None], rows, grad_slots, gate_table, up_block, down_block
    )
    returned = row_exchange(grad_rows)
    grad_down = matmul_left_t(expert_active, grad_result).astype(BF)
    grad_up = matmul_left_t(rows, grad_hidden).astype(BF)

    def paired(ours, theirs):
        return ours, swap(theirs)

    returned, expert_result, grad_up, grad_down = tie(
        (returned, expert_result, grad_up, grad_down)
    )
    result_back = row_exchange(expert_result.reshape(experts, CAP, width))
    result_back = result_back.reshape(slots, width)

    gate_slots = lax.dynamic_slice(
        returned, (0, CAP, (expert % IMAGES) * CAP), (experts, 2, CAP)
    ).astype(F32)
    gate_slots = (gate_slots[:, 0] + gate_slots[:, 1]).reshape(1, slots)
    gate_parts = jnp.stack(
        [jnp.sum(taken[i].astype(F32) * gate_slots, axis=1)[:tokens] for i in range(2)], axis=0
    )
    upper, lower = two_terms(gate_parts)
    tail = jnp.pad(jnp.concatenate([upper, lower], axis=0), ((0, 7), (0, width - tokens)))
    part = matmul(both_back, returned.reshape(experts * 48, width)).astype(BF)[:tokens]
    summed = col_sum(jnp.concatenate([part, tail], axis=0))
    up_pair = paired(*by_section(grad_up[:half], grad_up[half:]))
    down_pair = paired(*by_section(grad_down[:, :half], grad_down[:, half:]))
    summed, up_pair, down_pair = tie((summed, up_pair, down_pair))
    grad_gates = [
        jnp.pad(summed[tokens + i, :tokens] + summed[tokens + 2 + i, :tokens], (0, extra))
        for i in range(2)
    ]
    weighted = grad_gates[0] * gates[0] + grad_gates[1] * gates[1]
    grad_logits = shares * (
        hot[0] * grad_gates[0][:, None] + hot[1] * grad_gates[1][:, None] - weighted[:, None]
    )
    grad_router = lax.dot_general(
        grad_logits, second.astype(F32), (((0,), (0,)), ((), ())), precision=exact_mode
    )
    grad_second = jnp.pad(summed[:tokens], ((0, extra), (0, 0))) + lax.dot_general(
        grad_logits, gate_table.astype(F32), (((1,), (1,)), ((), ())), precision=exact_mode
    )
    grad_in, ours_b, theirs_b, grad_one_b, grad_two_b = run_attend_back(
        place, cotangent, grad_second, kept_second, gain_one[1], gain_two[1], gathered, 1
    )

    def joined(ours, theirs):
        return (ours.astype(F32) + theirs.astype(F32)).astype(BF).reshape(16, 48, half)

    def spread(gain):
        upper, lower = two_terms(gain.reshape(2, half))
        return jnp.concatenate([upper, lower], axis=0)

    def to_rows(*pieces):
        small = jnp.broadcast_to(pieces[-1][None], (16,) + pieces[-1].shape)
        return jnp.concatenate(pieces[:-1] + (small,), axis=1)

    def total(values):
        return jnp.sum(values.astype(F32), axis=0)

    def gain_total(values):
        values = total(values)
        return values[:2] + values[2:]

    ours, theirs = by_section(grad_router[:, :half], grad_router[:, half:])
    router_half = (ours + swap(theirs)).astype(BF)
    small = jnp.concatenate([spread(grad_one_b), spread(grad_two_b), router_half], axis=0)
    pieces_b, small_b = joined(ours_b, swap(theirs_b)), small
    grad_in, result_back = tie((grad_in, result_back))

    def columns_of(values, at):
        return lax.dynamic_slice_in_dim(values, at * quarter, quarter, 1)[:tokens]

    def own_columns(values):
        return columns_of(values, column)

    own = jnp.stack([section * 4 + column, (1 - section) * 4 + column])
    grad_second, *grad_fc = run_dense_back(own, grad_in, second_first, gathered)
    ours, theirs = grad_fc[0], swap(grad_fc[1])
    fc = (ours.astype(F32) + theirs.astype(F32)).astype(BF).reshape(16, 48, width)
    grad_second, fc, up_pair, down_pair, result_back = tie(
        (grad_second, fc, up_pair, down_pair, result_back)
    )
    sums_c = row_exchange(fc)
    grad_in, ours_a, theirs_a, grad_one_a, grad_two_a = run_attend_back(
        place, grad_in, grad_second, kept_first, gain_one[0], gain_two[0], gathered, 0
    )
    picked = gates[0][:, None] * matmul(taken[0], result_back) + gates[1][:, None] * matmul(
        taken[1], result_back
    )
    result = own_columns(middle) + own_columns(picked)
    for distance in (1, 2, 3):
        sent = columns_of(picked, (column + distance) % 4).astype(BF)
        result += from_col(sent, distance).astype(F32)
    result = result.astype(BF)

    ours_a, theirs_a, sums_c, result, up_pair, down_pair = tie(
        (ours_a, theirs_a, sums_c, result, up_pair, down_pair)
    )
    grad_start = own_columns(grad_in).astype(BF)
    small = jnp.concatenate([small_b, spread(grad_one_a), spread(grad_two_a)], axis=0)
    load = to_rows(pieces_b, joined(ours_a, swap(theirs_a)), small)
    load, sums_c, up_pair, down_pair = tie((load, sums_c, up_pair, down_pair))
    sum_up = up_pair[0].astype(F32) + up_pair[1].astype(F32)
    sum_down = down_pair[0].astype(F32) + down_pair[1].astype(F32)
    sums_a = row_exchange(load)


    shard_b, shard_a = total(sums_a[:, :48]), total(sums_a[:, 48:96])
    gains_b = jnp.concatenate([gain_total(sums_a[:, 96:100]), gain_total(sums_a[:, 100:104])], axis=0)
    gains_a = jnp.concatenate(
        [gain_total(sums_a[:, 120:124]), gain_total(sums_a[:, 124:128])], axis=0
    )
    mine, theirs = by_section(
        jnp.concatenate([shard_a, gains_a], axis=0), jnp.concatenate([shard_b, gains_b], axis=0)
    )
    theirs = swap(theirs)
    left, right = by_section(mine[:48], theirs[:48])
    gains = mine[48:] + theirs[48:]
    given = swap(jnp.where(first, result, grad_start))
    ends_out = jnp.stack(
        [jnp.where(first, grad_start, given), jnp.where(first, given, result)]
    )[None]
    return (
        ends_out,
        gains[:2].reshape(1, width),
        jnp.concatenate([left, right[:, : half - quarter]], axis=1)[None],
        right[:, half - quarter :].T[None],
        gains[2:].reshape(1, width),
        total(sums_c[:, :, :half]),
        total(sums_c[:, :, half:]).T,
        total(sums_a[:, 104:120]).T,
        sum_up[None],
        sum_down[None],
    )


def solution(mesh):
    placed = (
        P("section", None, "row", "col"),
        P("section", None),
        P("section", "row", "col"),
        P("section", "col", "row"),
        P("section", None),
        P("row", ("section", "col")),
        P(("section", "col"), "row"),
        P("section", None),
        P("row", "section", "col"),
        P("row", "col", "section"),
        P(None, "row", None),
    )
    return jax.shard_map(
        body,
        mesh=mesh,
        in_specs=placed,
        out_specs=(
            P("section", None, "row", "col"),
            P("section", None),
            P("section", "row", "col"),
            P("section", "col", "row"),
            P("section", None),
            P("row", ("section", "col")),
            P(("section", "col"), "row"),
            P("section", None),
            P("row", "section", "col"),
            P("row", "col", "section"),
        ),
        check_vma=False,
    )
```

```python
import jax
import jax.numpy as jnp
from jax import lax
from jax.experimental import pallas as pl
from jax.experimental.pallas import tpu as pltpu
from jax.sharding import PartitionSpec as P

HD = 64
SEQ = 197
CAP = 40

exact_mode = lax.Precision.HIGHEST
BF = jnp.bfloat16
F32 = jnp.float32


def swap(block):
    return lax.ppermute(block, "section", [(0, 1), (1, 0)])


def from_col(block, distance):
    return lax.ppermute(block, "col", [(i, (i + distance) % 4) for i in range(4)])


def matmul(left, right):
    return jnp.dot(left, right, preferred_element_type=F32)


def matmul_left_t(left, right):
    return lax.dot_general(left, right, (((0,), (0,)), ((), ())), preferred_element_type=F32)


def matmul_right_t(left, right):
    return lax.dot_general(left, right, (((1,), (1,)), ((), ())), preferred_element_type=F32)


def norm_parts(values):
    centre = values - jnp.mean(values, axis=-1, keepdims=True)
    spread = jnp.mean(centre * centre, axis=-1, keepdims=True)
    inverse = lax.rsqrt(spread + 1e-06)
    return centre * inverse, inverse


def norm_back(grad, gain, normed, inverse):
    scaled = grad * gain
    return inverse * (
        scaled
        - jnp.mean(scaled, axis=-1, keepdims=True)
        - normed * jnp.mean(scaled * normed, axis=-1, keepdims=True)
    )


def cdf_of(values):
    return 0.5 * (1.0 + lax.erf(values * 0.7071067811865476))


def gelu(values):
    return (values * cdf_of(values)).astype(BF)


def gelu_slope(values):
    return cdf_of(values) + values * jnp.exp(-0.5 * values * values) * 0.3989422804014327


def two_terms(values):
    upper = lax.optimization_barrier(values.astype(BF))
    lower = (values - upper.astype(F32)).astype(BF)
    return upper, lower


def col_sum(part):
    own = lax.optimization_barrier(part.astype(BF))
    parts = [own] + [from_col(own, distance) for distance in (1, 2, 3)]
    parts = [piece.astype(F32) for piece in parts]
    return (parts[0] + parts[2]) + (parts[1] + parts[3])


def row_exchange(values):
    return lax.all_to_all(values, "row", split_axis=0, concat_axis=0, tiled=True)


ROWS = 208
IMAGES = 8
GROUP = 192
SIDE = 768
PARAMS = pltpu.CompilerParams(vmem_limit_bytes=47 * 1024 * 1024)
SMALL = pltpu.CompilerParams(vmem_limit_bytes=24 * 1024 * 1024)


def cost(flops, size):
    return pl.CostEstimate(flops=int(flops), bytes_accessed=int(size), transcendentals=0)


def head(block, h, kind):
    at = h * GROUP + kind * HD
    return block[:, at : at + HD]


def key_shares(query, key):
    scores = matmul_right_t(key, query) * (HD ** (-0.5))
    keys = lax.broadcasted_iota(jnp.int32, scores.shape, 0)
    scores = jnp.where(keys < SEQ, scores, -1e30)
    shares = jnp.exp(scores - jnp.max(scores, axis=0, keepdims=True))
    return shares * (1.0 / jnp.sum(shares, axis=0, keepdims=True))


def attend_kernel(x_ref, one_ref, two_ref, w_ref, p_ref, o_ref, m_ref, mb_ref, c_ref, a_ref):
    step = pl.program_id(0)

    @pl.when(step == 0)
    def _():
        values = x_ref[...].astype(F32)
        normed, _ = norm_parts(values)
        a_ref[...] = (normed * one_ref[...]).astype(BF)
        m_ref[...] = values

    branch = 0.0
    for j in range(2):
        project = matmul(a_ref[...], w_ref[0, j]).astype(BF)
        p_ref[j] = project
        outs = [jnp.zeros((ROWS, HD), BF)]
        for h in range(3):
            shares = key_shares(head(project, h, 0), head(project, h, 1)).astype(BF)
            outs.append(matmul(head(project, h, 2).T, shares).astype(BF).T)
        mixed = jnp.concatenate(outs, axis=1)
        o_ref[j] = mixed
        branch += matmul_right_t(mixed, w_ref[0, j, :, 512:])
    m_ref[...] += branch

    @pl.when(step == 1)
    def _():
        mb_ref[...] = m_ref[...].astype(BF)
        normed, _ = norm_parts(mb_ref[...].astype(F32))
        c_ref[...] = (normed * two_ref[...]).astype(BF)


def attend_back_kernel(
    col_ref, g_ref, d_ref, m_ref, x_ref, one_ref, two_ref, p_ref, o_ref, w_ref,
    v_ref, ours_ref, theirs_ref, g1_ref, g2_ref, dm_ref, db_ref, acc_ref, dp_ref, a_ref,
):
    step = pl.program_id(0)

    @pl.when(step == 0)
    def _():
        normed, _ = norm_parts(x_ref[...].astype(F32))
        a_ref[...] = (normed * one_ref[...]).astype(BF)
        normed, inverse = norm_parts(m_ref[...].astype(F32))
        grad = d_ref[...]
        g2_ref[...] = jnp.sum(grad * normed, axis=0, keepdims=True)
        middle = g_ref[...].astype(F32) + norm_back(grad, two_ref[...], normed, inverse)
        dm_ref[...] = middle
        db_ref[...] = middle.astype(BF)
        acc_ref[...] = jnp.zeros_like(acc_ref)

    branch = db_ref[...]
    scale = HD ** (-0.5)
    total = 0.0
    for j in range(2):
        project = p_ref[j]
        grad_mixed = matmul(branch, w_ref[0, j, :, 512:]).astype(BF)
        grads = []
        for h in range(3):
            query, key, value = [head(project, h, kind) for kind in range(3)]
            grad_head = grad_mixed[:, (h + 1) * HD : (h + 2) * HD]
            shares = key_shares(query, key)
            grad_shares = matmul_right_t(value, grad_head)
            grad_value = matmul(shares.astype(BF), grad_head)
            grad_scores = shares * (
                grad_shares - jnp.sum(grad_shares * shares, axis=0, keepdims=True)
            )
            grad_scores = grad_scores.astype(BF)
            grads.append((scale * matmul(key.T, grad_scores)).astype(BF).T)
            grads.append((scale * matmul(grad_scores, query)).astype(BF))
            grads.append(grad_value.astype(BF))
        grads.append(jnp.zeros((ROWS, GROUP), BF))
        grad_project = jnp.concatenate(grads, axis=1)
        dp_ref[j] = grad_project
        total += matmul_right_t(grad_project, w_ref[0, j])
    acc_ref[...] += total

    @pl.when(step == col_ref[0] // 2)
    def _():
        place = col_ref[0] % 2
        grad_project = dp_ref[place]
        left = matmul_left_t(a_ref[...], grad_project[:, :512])
        right = matmul_left_t(a_ref[...], grad_project[:, 512:])
        right += matmul_left_t(branch, o_ref[place])
        low = left[:, :384].astype(BF)
        high = jnp.concatenate([left[:, 384:], right], axis=1).astype(BF)

        @pl.when(col_ref[1] == 0)
        def _():
            ours_ref[...] = low
            theirs_ref[...] = high

        @pl.when(col_ref[1] != 0)
        def _():
            ours_ref[...] = high
            theirs_ref[...] = low

    @pl.when(step == 1)
    def _():
        normed, inverse = norm_parts(x_ref[...].astype(F32))
        grad = acc_ref[...]
        g1_ref[...] = jnp.sum(grad * normed, axis=0, keepdims=True)
        v_ref[...] = dm_ref[...] + norm_back(grad, one_ref[...], normed, inverse)


def dense_kernel(c_ref, m_ref, w_ref, u_ref, acc_ref):
    step = pl.program_id(0)

    @pl.when(step == 0)
    def _():
        acc_ref[...] = m_ref[...]

    total = 0.0
    for j in range(2):
        active = gelu(matmul(c_ref[...], w_ref[0, j, :, :384]))
        total += matmul_right_t(active, w_ref[0, j, :, 384:])
    acc_ref[...] += total

    @pl.when(step == 3)
    def _():
        u_ref[...] = acc_ref[...].astype(BF)


def dense_back_kernel(own_ref, g_ref, c_ref, w_ref, d_ref, ours_ref, theirs_ref, pair_ref):
    step = pl.program_id(0)

    @pl.when(step == 0)
    def _():
        d_ref[...] = jnp.zeros_like(d_ref)

    grad = g_ref[...].astype(BF)
    total = 0.0
    for j in range(2):
        hidden = matmul(c_ref[...], w_ref[0, j, :, :384])
        active = gelu(hidden)
        grad_hidden = (matmul(grad, w_ref[0, j, :, 384:]) * gelu_slope(hidden)).astype(BF)
        total += matmul_right_t(grad_hidden, w_ref[0, j, :, :384])
        pair_ref[j, 0] = grad_hidden
        pair_ref[j, 1] = active
    d_ref[...] += total

    for place in range(2):

        @pl.when(step == own_ref[place] // 2)
        def _():
            at = own_ref[place] % 2
            gw_ref = (ours_ref, theirs_ref)[place]
            gw_ref[:, :384] = matmul_left_t(c_ref[...], pair_ref[at, 0]).astype(BF)
            gw_ref[:, 384:] = matmul_left_t(grad, pair_ref[at, 1]).astype(BF)


def expert_kernel(
    me_ref, x_ref, d_ref, table_ref, up_ref, down_ref, r_ref, back_ref, a_ref, dr_ref, dz_ref
):
    rows = x_ref[...]
    wide = d_ref[...].astype(F32)
    logits = matmul(rows, table_ref[...])
    shares = jnp.exp(logits - jnp.max(logits, axis=-1, keepdims=True))
    kinds = lax.broadcasted_iota(jnp.int32, shares.shape, 1)
    chosen = jnp.sum(jnp.where(kinds == me_ref[0], shares, 0.0), axis=-1, keepdims=True)
    gate = chosen / jnp.sum(shares, axis=-1, keepdims=True)
    hidden = matmul(rows, up_ref[...])
    active = gelu(hidden)
    result = matmul(active, down_ref[...])
    grad_result = (wide * gate).astype(BF)
    grad_active = matmul_right_t(grad_result, down_ref[...])
    grad_hidden = (grad_active * gelu_slope(hidden)).astype(BF)
    grad_rows = matmul_right_t(grad_hidden, up_ref[...])
    r_ref[...] = result.astype(BF)
    a_ref[...] = active
    dr_ref[...] = grad_result
    dz_ref[...] = grad_hidden
    products = wide * result
    products = sum(products[:, k * 128 : (k + 1) * 128] for k in range(SIDE // 128))
    products = jnp.concatenate([products, jnp.zeros((384 - IMAGES * CAP, 128), F32)], axis=0)
    sums = lax.dot_general(
        jnp.ones((8, 128), F32),
        products,
        (((1,), (1,)), ((), ())),
        preferred_element_type=F32,
        precision=exact_mode,
    )
    upper = sums.astype(BF).astype(F32)
    line = lax.broadcasted_iota(jnp.int32, sums.shape, 0)
    tail = jnp.where(line == 0, upper, jnp.where(line == 1, sums - upper, 0.0))
    tail = jnp.concatenate([tail, jnp.zeros((8, SIDE - 384), F32)], axis=1)
    for j in range(IMAGES):
        piece = jnp.concatenate([grad_rows[j * CAP : (j + 1) * CAP], tail], axis=0)
        back_ref[j] = piece.astype(BF)


def run_expert(expert, rows, grad_slots, table, up_block, down_block):
    slots = rows.shape[0]
    part = IMAGES * CAP
    moving = pl.BlockSpec((part, SIDE), lambda k, *_: (k, 0))
    spec = pltpu.PrefetchScalarGridSpec(
        num_scalar_prefetch=1,
        grid=(slots // part,),
        in_specs=[moving, moving, fixed(SIDE, 16), fixed(SIDE, SIDE), fixed(SIDE, SIDE)],
        out_specs=[
            moving,
            pl.BlockSpec((IMAGES, 48, SIDE), lambda k, *_: (k, 0, 0)),
            moving,
            moving,
            moving,
        ],
    )
    whole = pltpu.HBM((slots, SIDE), BF)
    return pl.pallas_call(
        expert_kernel,
        grid_spec=spec,
        out_shape=[whole, jax.ShapeDtypeStruct((16, 48, SIDE), BF), whole, whole, whole],
        compiler_params=SMALL,
        cost_estimate=cost(4e9, 1e7),
        name="expert",
    )(expert, rows, in_place(grad_slots), table, in_place(up_block), in_place(down_block))


def in_place(value):
    return pltpu.with_memory_space_constraint(value, pltpu.HBM)


def fixed(*shape):
    return pl.BlockSpec(shape, lambda k, *_: (0,) * len(shape))


def of_step(*shape):
    return pl.BlockSpec((2,) + shape, lambda k, *_: (k,) + (0,) * len(shape))


def run_attend(values, one, two, weights, layer):
    return pl.pallas_call(
        attend_kernel,
        grid=(2,),
        in_specs=[
            fixed(ROWS, SIDE),
            fixed(1, SIDE),
            fixed(1, SIDE),
            pl.BlockSpec((1, 2, SIDE, SIDE), lambda k: (layer, k, 0, 1)),
        ],
        out_specs=[
            of_step(ROWS, SIDE),
            of_step(ROWS, 256),
            fixed(ROWS, SIDE),
            fixed(ROWS, SIDE),
            fixed(ROWS, SIDE),
        ],
        out_shape=[
            pltpu.HBM((4, ROWS, SIDE), BF),
            pltpu.HBM((4, ROWS, 256), BF),
            jax.ShapeDtypeStruct((ROWS, SIDE), F32),
            pltpu.HBM((ROWS, SIDE), BF),
            jax.ShapeDtypeStruct((ROWS, SIDE), BF),
        ],
        scratch_shapes=[pltpu.VMEM((ROWS, SIDE), BF)],
        compiler_params=PARAMS,
        cost_estimate=cost(4e9, 8e6),
        name=f"attend_{layer}",
    )(values, one, two, weights)


def run_attend_back(column, grad_out, grad_second, kept, one, two, weights, layer):
    if layer == 0:
        kept = [in_place(value) for value in kept]
        grad_out, grad_second = in_place(grad_out), in_place(grad_second)
    values, project, mixed, middle = kept
    spec = pltpu.PrefetchScalarGridSpec(
        num_scalar_prefetch=1,
        grid=(2,),
        in_specs=[
            fixed(ROWS, SIDE),
            fixed(ROWS, SIDE),
            fixed(ROWS, SIDE),
            fixed(ROWS, SIDE),
            fixed(1, SIDE),
            fixed(1, SIDE),
            of_step(ROWS, SIDE),
            of_step(ROWS, 256),
            pl.BlockSpec((1, 2, SIDE, SIDE), lambda k, *_: (layer, k, 0, 1)),
        ],
        out_specs=[
            fixed(ROWS, SIDE),
            fixed(SIDE, 384),
            fixed(SIDE, 384),
            fixed(1, SIDE),
            fixed(1, SIDE),
        ],
        scratch_shapes=[
            pltpu.VMEM((ROWS, SIDE), F32),
            pltpu.VMEM((ROWS, SIDE), BF),
            pltpu.VMEM((ROWS, SIDE), F32),
            pltpu.VMEM((2, ROWS, SIDE), BF),
            pltpu.VMEM((ROWS, SIDE), BF),
        ],
    )
    return pl.pallas_call(
        attend_back_kernel,
        grid_spec=spec,
        out_shape=[
            pltpu.HBM((ROWS, SIDE), F32),
            jax.ShapeDtypeStruct((SIDE, 384), BF),
            jax.ShapeDtypeStruct((SIDE, 384), BF),
            jax.ShapeDtypeStruct((1, SIDE), F32),
            jax.ShapeDtypeStruct((1, SIDE), F32),
        ],
        compiler_params=PARAMS,
        cost_estimate=cost(8e9, 1e7),
        name=f"attend_back_{layer}",
    )(column, grad_out, grad_second, middle, values, one, two, project, mixed, weights)


def dense_block():
    return pl.BlockSpec((1, 2, SIDE, SIDE), lambda k, *_: (k // 2, k % 2, 0, 0))


def run_dense(second, middle, weights):
    return pl.pallas_call(
        dense_kernel,
        grid=(4,),
        in_specs=[fixed(ROWS, SIDE), fixed(ROWS, SIDE), dense_block()],
        out_specs=fixed(ROWS, SIDE),
        out_shape=jax.ShapeDtypeStruct((ROWS, SIDE), BF),
        scratch_shapes=[pltpu.VMEM((ROWS, SIDE), F32)],
        compiler_params=PARAMS,
        cost_estimate=cost(4e9, 1.2e7),
        name="dense",
    )(second, middle, weights)


def run_dense_back(own, grad, second, weights):
    spec = pltpu.PrefetchScalarGridSpec(
        num_scalar_prefetch=1,
        grid=(4,),
        in_specs=[fixed(ROWS, SIDE), fixed(ROWS, SIDE), dense_block()],
        out_specs=[fixed(ROWS, SIDE), fixed(SIDE, SIDE), fixed(SIDE, SIDE)],
        scratch_shapes=[pltpu.VMEM((2, 2, ROWS, 384), BF)],
    )
    return pl.pallas_call(
        dense_back_kernel,
        grid_spec=spec,
        out_shape=[
            pltpu.HBM((ROWS, SIDE), F32),
            jax.ShapeDtypeStruct((SIDE, SIDE), BF),
            jax.ShapeDtypeStruct((SIDE, SIDE), BF),
        ],
        compiler_params=PARAMS,
        cost_estimate=cost(8e9, 1.4e7),
        name="dense_back",
    )(own, in_place(grad), in_place(second), weights)


def body(ends, gain_attn, w_qkv, w_out, gain_ffn, w_fc1, w_fc2, router, w_up, w_down, routes):
    tokens = ends.shape[2]
    quarter = ends.shape[3]
    width = 4 * quarter
    half = width // 2
    experts = 16
    slots = experts * CAP
    extra = ROWS - tokens
    tie = lax.optimization_barrier
    section = lax.axis_index("section").astype(jnp.int32)
    first = section == 0
    column = lax.axis_index("col").astype(jnp.int32)
    expert = lax.axis_index("row").astype(jnp.int32)
    place = jnp.stack([column, section])

    def by_section(mine, theirs):
        return jnp.where(first, mine, theirs), jnp.where(first, theirs, mine)

    packed = jnp.concatenate([w_fc1, w_fc2.T, w_qkv[0], w_out[0].T], axis=1)
    gathered = lax.all_gather(packed, ("section", "col", "row"), axis=0, tiled=True)
    gathered = gathered.reshape(2, 4, width, 2 * width)

    kept = jnp.where(first, ends[0, 0], ends[0, 1])
    other = swap(jnp.where(first, ends[0, 1], ends[0, 0]))
    start, cotangent = by_section(kept, other)
    start = lax.all_gather(start, "col", axis=1, tiled=True)
    start, cotangent = tie((start, cotangent))
    cotangent = lax.all_gather(cotangent, "col", axis=1, tiled=True)
    start = jnp.pad(start, ((0, extra), (0, 0)))
    cotangent = jnp.pad(cotangent, ((0, extra), (0, 0)))
    choices = jnp.where(first, routes[0], routes[1])
    choices = jnp.pad(choices, ((0, extra), (0, 0)), constant_values=-1)
    gain_one = by_section(gain_attn, swap(gain_attn))
    gain_two = by_section(gain_ffn, swap(gain_ffn))
    gate_table = jnp.concatenate(by_section(router, swap(router)), axis=0)
    up_block = jnp.concatenate(by_section(w_up[0], swap(w_up[0])), axis=0)
    down_block = jnp.concatenate(by_section(w_down[0], swap(w_down[0])), axis=1)

    kinds = jnp.arange(experts, dtype=jnp.int32)
    hot = [(choices[:, i : i + 1] == kinds[None, :]).astype(F32) for i in range(2)]
    order = jnp.arange(ROWS, dtype=jnp.int32)
    before = (order[None, :] < order[:, None]).astype(BF)
    counts = matmul(before, (hot[0] + hot[1]).astype(BF))
    places = jnp.arange(slots, dtype=jnp.int32)
    taken = []
    targets_back = []
    for i in range(2):
        slot = jnp.sum(counts * hot[i], axis=1).astype(jnp.int32)
        target = choices[:, i] * CAP + slot
        targets_back.append(choices[:, i] * 48 + slot)
        taken.append((target[:, None] == places[None, :]).astype(BF))
    both = taken[0] + taken[1]
    places = jnp.arange(experts * 48, dtype=jnp.int32)
    both_back = sum((at[:, None] == places[None, :]).astype(BF) for at in targets_back)

    grad_slots = matmul_left_t(both, cotangent).astype(BF)
    grad_slots = row_exchange(grad_slots.reshape(experts, CAP, width)).reshape(slots, width)
    gathered, grad_slots, up_block, down_block = tie((gathered, grad_slots, up_block, down_block))

    project, mixed, middle, middle_low, second = run_attend(
        start, gain_one[0], gain_two[0], gathered, 0
    )
    kept_first = (start, project, mixed, middle_low)
    second_first = second
    handed = run_dense(second, middle, gathered)
    project, mixed, middle, middle_low, second = run_attend(
        handed, gain_one[1], gain_two[1], gathered, 1
    )
    kept_second = (handed, project, mixed, middle_low)
    sent = matmul_left_t(both, second).astype(BF)
    rows = row_exchange(sent.reshape(experts, CAP, width)).reshape(slots, width)
    shares = jax.nn.softmax(matmul(second, gate_table), axis=-1)
    gates = [jnp.sum(shares * hot[i], axis=1) for i in range(2)]

    expert_result, grad_rows, expert_active, grad_result, grad_hidden = run_expert(
        expert[None], rows, grad_slots, gate_table, up_block, down_block
    )
    returned = row_exchange(grad_rows)
    grad_down = matmul_left_t(expert_active, grad_result).astype(BF)
    grad_up = matmul_left_t(rows, grad_hidden).astype(BF)

    def paired(ours, theirs):
        return ours, swap(theirs)

    returned, expert_result, grad_up, grad_down = tie(
        (returned, expert_result, grad_up, grad_down)
    )
    result_back = row_exchange(expert_result.reshape(experts, CAP, width))
    result_back = result_back.reshape(slots, width)

    gate_slots = lax.dynamic_slice(
        returned, (0, CAP, (expert % IMAGES) * CAP), (experts, 2, CAP)
    ).astype(F32)
    gate_slots = (gate_slots[:, 0] + gate_slots[:, 1]).reshape(1, slots)
    gate_parts = jnp.stack(
        [jnp.sum(taken[i].astype(F32) * gate_slots, axis=1)[:tokens] for i in range(2)], axis=0
    )
    upper, lower = two_terms(gate_parts)
    tail = jnp.pad(jnp.concatenate([upper, lower], axis=0), ((0, 7), (0, width - tokens)))
    part = matmul(both_back, returned.reshape(experts * 48, width)).astype(BF)[:tokens]
    summed = col_sum(jnp.concatenate([part, tail], axis=0))
    up_pair = paired(*by_section(grad_up[:half], grad_up[half:]))
    down_pair = paired(*by_section(grad_down[:, :half], grad_down[:, half:]))
    summed, up_pair, down_pair = tie((summed, up_pair, down_pair))
    grad_gates = [
        jnp.pad(summed[tokens + i, :tokens] + summed[tokens + 2 + i, :tokens], (0, extra))
        for i in range(2)
    ]
    weighted = grad_gates[0] * gates[0] + grad_gates[1] * gates[1]
    grad_logits = shares * (
        hot[0] * grad_gates[0][:, None] + hot[1] * grad_gates[1][:, None] - weighted[:, None]
    )
    grad_router = lax.dot_general(
        grad_logits, second.astype(F32), (((0,), (0,)), ((), ())), precision=exact_mode
    )
    grad_second = jnp.pad(summed[:tokens], ((0, extra), (0, 0))) + lax.dot_general(
        grad_logits, gate_table.astype(F32), (((1,), (1,)), ((), ())), precision=exact_mode
    )
    grad_in, ours_b, theirs_b, grad_one_b, grad_two_b = run_attend_back(
        place, cotangent, grad_second, kept_second, gain_one[1], gain_two[1], gathered, 1
    )

    def joined(ours, theirs):
        return (ours.astype(F32) + theirs.astype(F32)).astype(BF).reshape(16, 48, half)

    def spread(gain):
        upper, lower = two_terms(gain.reshape(2, half))
        return jnp.concatenate([upper, lower], axis=0)

    def to_rows(*pieces):
        small = jnp.broadcast_to(pieces[-1][None], (16,) + pieces[-1].shape)
        return jnp.concatenate(pieces[:-1] + (small,), axis=1)

    def total(values):
        return jnp.sum(values.astype(F32), axis=0)

    def gain_total(values):
        values = total(values)
        return values[:2] + values[2:]

    ours, theirs = by_section(grad_router[:, :half], grad_router[:, half:])
    router_half = (ours + swap(theirs)).astype(BF)
    small = jnp.concatenate([spread(grad_one_b), spread(grad_two_b), router_half], axis=0)
    pieces_b, small_b = joined(ours_b, swap(theirs_b)), small
    grad_in, result_back = tie((grad_in, result_back))

    def columns_of(values, at):
        return lax.dynamic_slice_in_dim(values, at * quarter, quarter, 1)[:tokens]

    def own_columns(values):
        return columns_of(values, column)

    own = jnp.stack([section * 4 + column, (1 - section) * 4 + column])
    grad_second, *grad_fc = run_dense_back(own, grad_in, second_first, gathered)
    ours, theirs = grad_fc[0], swap(grad_fc[1])
    fc = (ours.astype(F32) + theirs.astype(F32)).astype(BF).reshape(16, 48, width)
    grad_second, fc, up_pair, down_pair, result_back = tie(
        (grad_second, fc, up_pair, down_pair, result_back)
    )
    sums_c = row_exchange(jnp.concatenate([fc, pieces_b], axis=2))
    grad_in, ours_a, theirs_a, grad_one_a, grad_two_a = run_attend_back(
        place, grad_in, grad_second, kept_first, gain_one[0], gain_two[0], gathered, 0
    )
    picked = gates[0][:, None] * matmul(taken[0], result_back) + gates[1][:, None] * matmul(
        taken[1], result_back
    )
    result = own_columns(middle) + own_columns(picked)
    for distance in (1, 2, 3):
        sent = columns_of(picked, (column + distance) % 4).astype(BF)
        result += from_col(sent, distance).astype(F32)
    result = result.astype(BF)

    ours_a, theirs_a, sums_c, result, up_pair, down_pair = tie(
        (ours_a, theirs_a, sums_c, result, up_pair, down_pair)
    )
    grad_start = own_columns(grad_in).astype(BF)
    small = jnp.concatenate([small_b, spread(grad_one_a), spread(grad_two_a)], axis=0)
    load = to_rows(joined(ours_a, swap(theirs_a)), small)
    load, sums_c, up_pair, down_pair = tie((load, sums_c, up_pair, down_pair))
    sum_up = up_pair[0].astype(F32) + up_pair[1].astype(F32)
    sum_down = down_pair[0].astype(F32) + down_pair[1].astype(F32)
    sums_a = row_exchange(load)


    shard_b, shard_a = total(sums_c[:, :, width:]), total(sums_a[:, :48])
    gains_b = jnp.concatenate([gain_total(sums_a[:, 48:52]), gain_total(sums_a[:, 52:56])], axis=0)
    gains_a = jnp.concatenate(
        [gain_total(sums_a[:, 72:76]), gain_total(sums_a[:, 76:80])], axis=0
    )
    mine, theirs = by_section(
        jnp.concatenate([shard_a, gains_a], axis=0), jnp.concatenate([shard_b, gains_b], axis=0)
    )
    theirs = swap(theirs)
    left, right = by_section(mine[:48], theirs[:48])
    gains = mine[48:] + theirs[48:]
    given = swap(jnp.where(first, result, grad_start))
    ends_out = jnp.stack(
        [jnp.where(first, grad_start, given), jnp.where(first, given, result)]
    )[None]
    return (
        ends_out,
        gains[:2].reshape(1, width),
        jnp.concatenate([left, right[:, : half - quarter]], axis=1)[None],
        right[:, half - quarter :].T[None],
        gains[2:].reshape(1, width),
        total(sums_c[:, :, :half]),
        total(sums_c[:, :, half:width]).T,
        total(sums_a[:, 56:72]).T,
        sum_up[None],
        sum_down[None],
    )


def solution(mesh):
    placed = (
        P("section", None, "row", "col"),
        P("section", None),
        P("section", "row", "col"),
        P("section", "col", "row"),
        P("section", None),
        P("row", ("section", "col")),
        P(("section", "col"), "row"),
        P("section", None),
        P("row", "section", "col"),
        P("row", "col", "section"),
        P(None, "row", None),
    )
    return jax.shard_map(
        body,
        mesh=mesh,
        in_specs=placed,
        out_specs=(
            P("section", None, "row", "col"),
            P("section", None),
            P("section", "row", "col"),
            P("section", "col", "row"),
            P("section", None),
            P("row", ("section", "col")),
            P(("section", "col"), "row"),
            P("section", None),
            P("row", "section", "col"),
            P("row", "col", "section"),
        ),
        check_vma=False,
    )
```
